128 devices in a mesh: dp: 4 (over y), expert: 32 (over z, x, core).
Axes of the slice: x: 4, y: 4, z: 4, core: 2. Of those that a mesh axis runs over, the one named last changes fastest.
Arguments:
- grad_out: bfloat16 [32768, 4096], P(('dp', 'expert')), may hold values from -6 to 6
- expert_ids: int32 [32768, 8], P(('dp', 'expert')), may hold values from 0 to 63, all different within a row; in each aligned block of 256 rows (0 to 255, 256 to 511, ...) at most 36 rows name the same one
- route_weights: bfloat16 [32768, 8], P(('dp', 'expert')), may hold values from 0.099609375 to 1
- gate_values: bfloat16 [4, 64, 1152, 768], P('dp', 'expert'), may hold values from -5 to 5
- up_values: bfloat16 [4, 64, 1152, 768], P('dp', 'expert'), may hold values from -5 to 5
- w_down: bfloat16 [64, 768, 4096], P('expert', None, 'dp'), as said below
Outputs:
- grad_gate: bfloat16 [4, 64, 1152, 768], P('dp', 'expert')
- grad_up: bfloat16 [4, 64, 1152, 768], P('dp', 'expert')
- grad_down: bfloat16 [64, 768, 4096], P('expert', None, 'dp')
- grad_route: float32 [32768, 8], P(('dp', 'expert'))
The draws below stay inside these ranges and needn't reach their ends.
Inputs may be any that keep to these rules, and one draw needn't show every extreme that they name: `expert_ids`: each token names 8 different experts. Among the tokens of one device no expert is named by more than 36 tokens, a bound that some block reaches. `w_down`: rows of the experts' weights and its columns have different scales.
All inputs are finite; a program needn't handle non-finite values.
Results may differ from the reference program's by a relative error of at most 0.015.
Values may be sent and summed in bfloat16 or wider, within the bound.
No kernel may reach another device: no remote copies, remote signals or barrier semaphores. Data moves between devices by JAX's collectives and lax.ppermute only.
A program may use at most 256 MiB of HBM per device.

```python
import math
import jax
import jax.numpy as jnp
import numpy as np
from jax import lax

D = 4096
H = 768
TOP = 8
TOK_DEV = 256
EXPERTS = 64
CAP = 36
SLOTS = 1152
TOKENS = 32768
N_DP = 4
N_EXPERT = 32


def draw_w_down(key, part):
    key = jax.random.fold_in(key, 7)
    first_key, second_key, third_key, common_key, order_key, level_key = jax.random.split(key, 6)
    base = jax.random.normal(first_key, (EXPERTS, H, D), jnp.float32)
    row_scale = jnp.exp(jax.random.uniform(second_key, (EXPERTS, H, 1), jnp.float32, math.log(0.3), math.log(3.0)))
    tie_most = 0.75
    common = jnp.abs(jax.random.normal(common_key, (EXPERTS, H // 4, 1, D), jnp.float32))
    common = jnp.broadcast_to(common, (EXPERTS, H // 4, 4, D)).reshape(EXPERTS, H, D)
    ranks = jax.vmap(lambda one_key: jax.random.permutation(one_key, 8))(jax.random.split(order_key, EXPERTS))
    jitter = jax.random.uniform(level_key, (EXPERTS, 8), jnp.float32, 0.1, 0.9)
    tie_block = (ranks.astype(jnp.float32) + jitter) / 8.0 * tie_most
    tie_column = jnp.repeat(tie_block, D // 8, axis=1)[:, None, :]
    shaped = jnp.sign(base) * ((1.0 - tie_column) * jnp.abs(base) + tie_column * common)
    column_scale = jnp.exp(jax.random.uniform(third_key, (EXPERTS, 1, D), jnp.float32, math.log(0.3), math.log(3.0)))
    rising = jnp.exp(math.log(3.0) * (jnp.arange(D, dtype=jnp.float32) / D - 0.5))
    values = shaped * row_scale * column_scale * rising[None, None, :] / (2.0 * math.sqrt(H))
    return values.astype(jnp.bfloat16)


def block_levels(rng, dims, pieces, low, high):
    loudness, own = 1.0, jax.random.fold_in(rng, 6)
    for axis_at, blocks in pieces:
        draws = jnp.exp(jax.random.uniform(jax.random.fold_in(own, axis_at), (blocks,), jnp.float32, low / len(pieces), high / len(pieces)))
        loudness = loudness * jnp.repeat(draws, dims[axis_at] // blocks).reshape([-1 if axis == axis_at else 1 for axis in range(len(dims))])
    return loudness


def deal_out(stream_key, own, number, rows, count, top, limit, slope):
    ranking = jax.random.permutation(stream_key, count)
    packed, usual = portions_of(count, rows * top, limit, slope, True), portions_of(count, rows * top, limit, slope, False)
    places = jnp.arange(count)

    def named(tallies, rotation):
        used = int((tallies > 0).sum())
        fixed = max(1, used // 4)
        moved = fixed + (places - fixed + rotation * (used - fixed)) % max(1, count - fixed)
        return jnp.zeros((count,), jnp.int32).at[ranking[jnp.where(places < fixed, places, moved)]].set(jnp.asarray(tallies, jnp.int32))

    tallies = jnp.where(number % 4 == 0, named(packed, number // 4), named(usual, number - number // 4 - 1))
    mixed = jax.random.permutation(jax.random.fold_in(own, 3), count)
    donor, sink = mixed[0:count // 2 * 2:2], mixed[1:count // 2 * 2:2]
    room = jnp.minimum(tallies[donor] - 1, limit - tallies[sink]) // 2
    room = jnp.where((donor == ranking[0]) | (sink == ranking[0]) | (tallies[sink] == 0), 0, jnp.maximum(room, 0))
    moved = jax.random.randint(jax.random.fold_in(own, 4), (count // 2,), 0, 1 << 20) % (room + 1)
    tallies = tallies.at[donor].add(-moved).at[sink].add(moved)
    members = jnp.searchsorted(jnp.cumsum(tallies), jnp.arange(rows * top), side="right").astype(jnp.int32)
    listing = members.reshape(top, rows).T
    listing = listing[jax.random.permutation(jax.random.fold_in(own, 1), rows)]
    rotation = jax.random.randint(jax.random.fold_in(own, 2), (rows, 1), 0, top)
    return jnp.take_along_axis(listing, (jnp.arange(top)[None, :] + rotation) % top, axis=1)


def portions_of(count, total, limit, skew, full):
    portions = [(1 << 20) // math.isqrt(grade ** skew) + 1 for grade in range(1, count + 1)]
    largest = limit if full else min(limit, max(-(-total // count), total * portions[0] // sum(portions)))
    least = 1 if total - largest >= count - 1 else 0
    holding, spare = [largest] + [least] * (count - 1), total - largest - least * (count - 1)
    while spare > 0:
        movable = [i for i in range(1, count) if holding[i] < largest] or [i for i in range(1, count) if holding[i] < limit]
        whole, budget = sum([portions[i] for i in movable]), spare
        for i in movable:
            addition = min(limit - holding[i], max(1, budget * portions[i] // whole), spare)
            holding[i] = holding[i] + addition
            spare = spare - addition
    return np.array(holding)


def noise(own_key, shape, spread, most, shards=(), kind=jnp.bfloat16):
    drawn = spread * jax.random.normal(own_key, shape, jnp.float32)
    if shards:
        drawn = drawn * block_levels(own_key, shape, shards, -0.22, 0.18)
    return jnp.clip(drawn, -most, most).astype(kind)


def setup_inputs(seed: int = 0) -> dict:
    splits = jax.random.split(jax.random.key(seed), 7)
    grad_out = noise(splits[0], (TOKENS, D), 1.0, 6.0, ((0, 128),))
    expert_ids_keys = jax.random.split(jax.random.fold_in(splits[1], 1), TOKENS // TOK_DEV)
    expert_ids_turns = jax.random.permutation(jax.random.fold_in(splits[1], 3), TOKENS // TOK_DEV)
    expert_ids = jax.vmap(lambda own, number: deal_out(jax.random.fold_in(splits[1], 2), own, number, TOK_DEV, EXPERTS, TOP, CAP, 0))(expert_ids_keys, expert_ids_turns).reshape((TOKENS, TOP))
    route_weights = jnp.clip(0.099609375 + 0.9003906 * jax.random.uniform(splits[2], (TOKENS, TOP), jnp.float32) ** block_levels(splits[2], (TOKENS, TOP), ((0, 128),), -0.2, 0.2), 0.099609375, 1.0).astype(jnp.bfloat16)
    gate_values = noise(splits[3], (N_DP, EXPERTS, SLOTS, H), 1.0, 5.0, ((0, 4), (1, 32)))
    up_values = noise(splits[4], (N_DP, EXPERTS, SLOTS, H), 1.0, 5.0, ((0, 4), (1, 32)))
    w_down = draw_w_down(jax.random.fold_in(splits[6], 71), 0)
    return {"grad_out": grad_out, "expert_ids": expert_ids, "route_weights": route_weights, "gate_values": gate_values, "up_values": up_values, "w_down": w_down}


epsilon = 1e-6


def shrink_groups(weight):
    dense_values = weight.astype(jnp.float32)
    block_count, hidden_units, column_total = dense_values.shape
    magnitude = jnp.abs(dense_values).reshape(block_count, hidden_units // 4, 4, column_total)
    lower_one = jnp.minimum(magnitude[:, :, 0], magnitude[:, :, 1])
    upper_one = jnp.maximum(magnitude[:, :, 0], magnitude[:, :, 1])
    lower_two = jnp.minimum(magnitude[:, :, 2], magnitude[:, :, 3])
    upper_two = jnp.maximum(magnitude[:, :, 2], magnitude[:, :, 3])
    second = jnp.minimum(jnp.maximum(lower_one, lower_two), jnp.minimum(upper_one, upper_two))
    kept_part = jnp.maximum(magnitude - second[:, :, None, :], 0.0).reshape(block_count, hidden_units, column_total)
    return dense_values, jnp.sign(dense_values) * kept_part


def block_places(flat_ids):
    onehot = (flat_ids[:, None] == jnp.arange(EXPERTS, dtype=jnp.int32)[None, :]).astype(jnp.int32)
    before = jnp.cumsum(onehot, axis=0) - onehot
    slot_index = jnp.sum(before * onehot, axis=1).astype(jnp.int32)
    return flat_ids * CAP + slot_index


def reference(grad_out, expert_ids, route_weights, gate_values, up_values, w_down):
    blocks = N_DP * N_EXPERT
    per_block = expert_ids.reshape(blocks, TOK_DEV * TOP)
    local_place = jax.vmap(block_places)(per_block)
    block_index = jnp.arange(blocks, dtype=jnp.int32)[:, None]
    group_index = block_index // N_EXPERT
    member = block_index % N_EXPERT
    expert_of = local_place // CAP
    slot_of = local_place % CAP
    global_place = ((group_index * EXPERTS + expert_of) * SLOTS + member * CAP + slot_of).reshape(-1).astype(jnp.int32)
    place_total = N_DP * EXPERTS * SLOTS
    source_row = jnp.zeros((place_total,), jnp.int32).at[global_place].set(jnp.arange(TOKENS * TOP, dtype=jnp.int32))
    filled_mask = jnp.zeros((place_total,), jnp.int32).at[global_place].set(1)
    source_row = source_row.reshape(N_DP, EXPERTS, SLOTS)
    filled_mask = filled_mask.reshape(N_DP, EXPERTS, SLOTS)
    flat_weights = route_weights.reshape(-1)

    def one_expert(expert):
        dense_values, shrunk = shrink_groups(w_down[expert][None])
        inner_sum = jnp.sum(dense_values * shrunk)
        squares = jnp.sum(shrunk * shrunk)
        factor = inner_sum / (squares + epsilon)
        effective = (factor * shrunk[0]).astype(jnp.bfloat16)
        grad_sum = jnp.zeros((H, D), jnp.float32)
        gate_list = []
        up_list = []
        score_list = []
        for group in range(N_DP):
            row_index = source_row[group, expert]
            live = filled_mask[group, expert] > 0
            arrived = jnp.where(live[:, None], grad_out[row_index // TOP], jnp.zeros((), jnp.bfloat16))
            slot_weight = jnp.where(live, flat_weights[row_index], jnp.zeros((), jnp.bfloat16)).astype(jnp.float32)
            slot_grads = jnp.dot(arrived, effective.T, preferred_element_type=jnp.float32)
            gate_float = gate_values[group, expert].astype(jnp.float32)
            up_float = up_values[group, expert].astype(jnp.float32)
            sigmoid_gate = jax.nn.sigmoid(gate_float)
            activated = gate_float * sigmoid_gate
            product = activated * up_float
            scaled = slot_weight[:, None] * slot_grads
            gate_list.append((scaled * up_float * sigmoid_gate * (1.0 + gate_float * (1.0 - sigmoid_gate))).astype(jnp.bfloat16))
            up_list.append((scaled * activated).astype(jnp.bfloat16))
            score_list.append(jnp.sum(slot_grads * product, axis=1))
            weighted = (slot_weight[:, None] * product).astype(jnp.bfloat16)
            partial_grad = jnp.dot(weighted.T, arrived, preferred_element_type=jnp.float32)
            partial_grad = lax.optimization_barrier(partial_grad.astype(jnp.bfloat16)).astype(jnp.float32)
            grad_sum = grad_sum + partial_grad
        grad_weight = (factor * grad_sum).astype(jnp.bfloat16)
        return jnp.stack(gate_list), jnp.stack(up_list), grad_weight, jnp.stack(score_list)

    gates, ups, downs, scores = lax.map(one_expert, jnp.arange(EXPERTS, dtype=jnp.int32))
    grad_gate = jnp.transpose(gates, (1, 0, 2, 3))
    grad_up = jnp.transpose(ups, (1, 0, 2, 3))
    score_flat = jnp.transpose(scores, (1, 0, 2)).reshape(-1)
    grad_route = score_flat[global_place].reshape(TOKENS, TOP)
    return grad_gate, grad_up, downs, grad_route
```

```python
import functools

import jax
import jax.numpy as jnp
from jax import lax
from jax.experimental import pallas as pl
from jax.experimental.pallas import tpu as pltpu
from jax.sharding import PartitionSpec as P

epsilon = 1e-06

D = 4096
H = 768
TOP = 8
TOK = 256
CAP = 36
SLOTS = 1152
NZ = NX = 4
NDP = 4
PART = 2 * CAP
SEG = NZ * PART
UNIT = 256
CHUNKS = 2
SHIFTS = (0, 1, 3, 2)
VMEM_LIMIT = 56 * 1024 * 1024


def member(z, x, core):
    return ((z % NZ) * NX + (x % NX)) * 2 + core


def pairs(first_axis, shift, swap):
    out = []
    for z in range(NZ):
        for x in range(NX):
            for core in range(2):
                along_z = (core == 0) == first_axis
                to = (z + shift, x) if along_z else (z, x + shift)
                out.append((member(z, x, core), member(*to, core ^ swap)))
    return out


def params(**kw):
    return pltpu.CompilerParams(vmem_limit_bytes=VMEM_LIMIT, **kw)


def cost(flops, nbytes, trans=0):
    return pl.CostEstimate(flops=int(flops), bytes_accessed=int(nbytes), transcendentals=int(trans))


def shrink_kernel(w_ref, out_ref, sums_ref):
    dense = w_ref[0].astype(jnp.float32)
    row = lax.broadcasted_iota(jnp.int32, dense.shape, 0)
    odd = (row & 1) == 1
    high = (row & 2) == 2

    def across(value, step, upper):
        return jnp.where(
            upper, pltpu.roll(value, step, 0), pltpu.roll(value, value.shape[0] - step, 0)
        )

    mag = jnp.abs(dense)
    other = across(mag, 1, odd)
    low, up = jnp.minimum(mag, other), jnp.maximum(mag, other)
    second = jnp.minimum(
        jnp.maximum(low, across(low, 2, high)), jnp.minimum(up, across(up, 2, high))
    )
    kept = jnp.maximum(mag - second, 0.0)
    shrunk = jnp.where(dense < 0.0, -kept, kept)
    out_ref[0, 0] = shrunk.astype(jnp.bfloat16)

    def fold(value):
        value = jnp.sum(value.reshape(H // 8, 8, UNIT), axis=0)
        return value[:, :128] + value[:, 128:]

    sums_ref[0, 0, 0] = fold(dense * shrunk)
    sums_ref[0, 0, 1] = fold(shrunk * shrunk)


def shrink(w_down):
    return pl.pallas_call(
        shrink_kernel,
        grid=(4, 2),
        in_specs=[pl.BlockSpec((1, H, UNIT), lambda q, e: (e, 0, q))],
        out_specs=[
            pl.BlockSpec((1, 1, H, UNIT), lambda q, e: (q, e, 0, 0)),
            pl.BlockSpec((1, 1, 2, 8, 128), lambda q, e: (q, e, 0, 0, 0)),
        ],
        out_shape=[
            jax.ShapeDtypeStruct((4, 2, H, UNIT), jnp.bfloat16),
            jax.ShapeDtypeStruct((4, 2, 2, 8, 128), jnp.float32),
        ],
        compiler_params=params(),
        cost_estimate=cost(2 * H * 1024 * 30, 2 * 2 * H * 1024 * 2),
        name="shrink",
    )(w_down)


def route_kernel(ids_ref, weights_ref, table_ref, rank_ref):
    expert = lax.broadcasted_iota(jnp.int32, (64, TOK), 0)
    named = jnp.zeros((64, TOK), jnp.float32)
    weight = jnp.zeros((64, TOK), jnp.float32)
    for k in range(TOP):
        hit = ids_ref[k : k + 1, :] == expert
        named = jnp.where(hit, 1.0, named)
        weight = jnp.where(hit, weights_ref[k : k + 1, :], weight)
    earlier = lax.broadcasted_iota(jnp.int32, (TOK, TOK), 0) < lax.broadcasted_iota(
        jnp.int32, (TOK, TOK), 1
    )
    rank = jnp.dot(
        named.astype(jnp.bfloat16),
        earlier.astype(jnp.bfloat16),
        preferred_element_type=jnp.float32,
    )
    rank = jnp.where(named > 0.0, rank, -1.0)
    rank_ref[...] = rank
    lane = lax.broadcasted_iota(jnp.int32, (64, 128), 1)
    slot_weight = jnp.zeros((64, 128), jnp.float32)
    for slot in range(CAP):
        one = jnp.sum(jnp.where(rank == float(slot), weight, 0.0), axis=1, keepdims=True)
        slot_weight = jnp.where(lane == slot, one, slot_weight)
    table_ref[:, :TOK] = rank.astype(jnp.bfloat16)
    table_ref[:, TOK:] = slot_weight.astype(jnp.bfloat16)


def route(ids, weights):
    return pl.pallas_call(
        route_kernel,
        out_shape=[
            jax.ShapeDtypeStruct((64, TOK + 128), jnp.bfloat16),
            jax.ShapeDtypeStruct((64, TOK), jnp.float32),
        ],
        compiler_params=params(),
        name="route",
    )(ids.T, weights.astype(jnp.float32).T)


def back_kernel(ids_ref, rank_ref, score_ref, out_ref):
    expert = lax.broadcasted_iota(jnp.int32, (64, TOK), 0)
    rank = rank_ref[...]
    score = jnp.zeros((64, TOK), jnp.float32)
    for slot in range(CAP):
        score = jnp.where(rank == float(slot), score_ref[:, slot : slot + 1], score)
    for k in range(TOP):
        hit = ids_ref[k : k + 1, :] == expert
        out_ref[k : k + 1, :] = jnp.sum(jnp.where(hit, score, 0.0), axis=0, keepdims=True)


def back(ids, rank, score):
    out = pl.pallas_call(
        back_kernel,
        out_shape=jax.ShapeDtypeStruct((TOP, TOK), jnp.float32),
        compiler_params=params(),
        name="back",
    )(ids.T, rank, score)
    return out.T


def pick_kernel(chunk, where_ref, rank_ref, *refs):
    blocks, outs = refs[:4], refs[4:12]
    tokens, onehot, picked, sems = refs[12:]
    step = pl.program_id(0)

    @pl.when(step == 0)
    def _():
        copies = [
            pltpu.make_async_copy(blocks[i].at[chunk], tokens.at[where_ref[i]], sems.at[i])
            for i in range(4)
        ]
        for copy in copies:
            copy.start()
        row = lax.broadcasted_iota(jnp.int32, (PART, 2 * TOK), 0)
        lane = lax.broadcasted_iota(jnp.int32, (PART, 2 * TOK), 1)
        second = row >= CAP
        slot = jnp.where(second, row - CAP, row)
        slot = jnp.where(second == (lane >= TOK), slot, -2).astype(jnp.float32)
        for block in range(4):
            for i in range(16):
                hit = slot == rank_ref[block, i : i + 1, :]
                onehot[block, i * PART : (i + 1) * PART, :] = jnp.where(hit, 1.0, 0.0).astype(
                    jnp.bfloat16
                )
        for copy in copies:
            copy.wait()

    columns = pl.ds(pl.multiple_of(step * UNIT, UNIT), UNIT)
    for block in range(4):
        picked[block] = jnp.dot(
            onehot[block], tokens[block, :, columns], preferred_element_type=jnp.float32
        )
    for i in range(16):
        rows = pl.ds(i * PART, PART)
        joined = jnp.concatenate([picked[block, rows, :] for block in range(4)], axis=0)
        outs[i // 2][i % 2] = joined.astype(jnp.bfloat16)


def pick(chunk, where, rank, blocks):
    any_spec = pl.BlockSpec(memory_space=pl.ANY)
    return pl.pallas_call(
        functools.partial(pick_kernel, chunk),
        grid_spec=pltpu.PrefetchScalarGridSpec(
            num_scalar_prefetch=1,
            grid=(4,),
            in_specs=[pl.BlockSpec((4, 16, 2 * TOK), lambda n, s: (0, 0, 0))] + [any_spec] * 4,
            out_specs=[pl.BlockSpec((2, SEG, UNIT), lambda n, s: (0, 0, n))] * 8,
            scratch_shapes=[
                pltpu.VMEM((4, 2 * TOK, 1024), jnp.bfloat16),
                pltpu.VMEM((4, 16 * PART, 2 * TOK), jnp.bfloat16),
                pltpu.VMEM((4, 16 * PART, UNIT), jnp.float32),
                pltpu.SemaphoreType.DMA((4,)),
            ],
        ),
        out_shape=[jax.ShapeDtypeStruct((2, SEG, 1024), jnp.bfloat16)] * 8,
        compiler_params=params(),
        cost_estimate=cost(2 * 4 * 1152 * 512 * 1024, 4 * 1024 * 1024 + 8 * 2 * SEG * 1024 * 2),
        name=f"pick{chunk}",
    )(where, rank, *blocks)


def weigh_kernel(gate_ref, up_ref, weight_ref, out_ref):
    gate = gate_ref[0].astype(jnp.float32)
    up = up_ref[0].astype(jnp.float32)
    sig = 1.0 / (1.0 + jnp.exp(-gate))
    value = weight_ref[0] * (gate * sig * up)
    out_ref[1, 0] = value.astype(jnp.bfloat16).T
    turned = jnp.concatenate(
        [
            value[(z * NX + x) * PART : (z * NX + x + 1) * PART]
            for x in range(NX)
            for z in range(NZ)
        ],
        axis=0,
    )
    out_ref[0, 0] = turned.astype(jnp.bfloat16).T


def weigh(gate, up, slot_weight):
    wide = 256
    return pl.pallas_call(
        weigh_kernel,
        grid=(2, H // wide),
        in_specs=[
            pl.BlockSpec((1, SLOTS, wide), lambda e, n: (e, 0, n)),
            pl.BlockSpec((1, SLOTS, wide), lambda e, n: (e, 0, n)),
            pl.BlockSpec((1, SLOTS, 1), lambda e, n: (e, 0, 0)),
        ],
        out_specs=pl.BlockSpec((2, 1, wide, SLOTS), lambda e, n: (0, e, n, 0)),
        out_shape=jax.ShapeDtypeStruct((2, 2, H, SLOTS), jnp.bfloat16),
        compiler_params=params(),
        cost_estimate=cost(2 * SLOTS * H * 20, 2 * SLOTS * H * 8, 2 * SLOTS * H),
        name="weigh",
    )(gate, up, slot_weight)


def row_copies(where_ref, buffers, group, e, rows, sems):
    return [
        pltpu.make_async_copy(
            buffers[4 * group + i].at[e],
            rows.at[pl.ds(pl.multiple_of(where_ref[4 * group + i] * SEG, SEG), SEG)],
            sems.at[i],
        )
        for i in range(4)
    ]


def partial_kernel(where_ref, weighted_ref, *refs):
    buffers, out_ref, rows, sems = refs[:8], refs[8], refs[9], refs[10]
    step = pl.program_id(0)
    slot = step & 1

    def fetch(at, into):
        for i in range(4):
            @pl.when(at == i)
            def _(i=i):
                for copy in row_copies(where_ref, buffers, i // 2, i % 2, rows.at[into], sems.at[into]):
                    copy.start()

    @pl.when(step == 0)
    def _():
        fetch(step, 0)

    @pl.when(step < 3)
    def _():
        fetch(step + 1, 1 - slot)

    for copy in row_copies(where_ref, buffers, 0, 0, rows.at[slot], sems.at[slot]):
        copy.wait()
    for j in range(NDP):
        out_ref[j, 0, 0] = jnp.dot(
            weighted_ref[0, 0],
            rows[slot, :, j * UNIT : (j + 1) * UNIT],
            preferred_element_type=jnp.float32,
        ).astype(jnp.bfloat16)


def partial(chunk, where, weighted, buffers):
    any_spec = pl.BlockSpec(memory_space=pl.ANY)
    return pl.pallas_call(
        partial_kernel,
        grid_spec=pltpu.PrefetchScalarGridSpec(
            num_scalar_prefetch=1,
            grid=(4,),
            in_specs=[pl.BlockSpec((1, 1, H, SLOTS), lambda n, s: (s[8 + n // 2], n % 2, 0, 0))]
            + [any_spec] * 8,
            out_specs=pl.BlockSpec(
                (NDP, 1, 1, H, UNIT), lambda n, s: (0, s[8 + n // 2], n % 2, 0, 0)
            ),
            scratch_shapes=[
                pltpu.VMEM((2, SLOTS, 1024), jnp.bfloat16),
                pltpu.SemaphoreType.DMA((2, 4)),
            ],
        ),
        out_shape=jax.ShapeDtypeStruct((NDP, 2, 2, H, UNIT), jnp.bfloat16),
        compiler_params=params(),
        cost_estimate=cost(2 * 2 * SLOTS * H * 2048, 2 * SLOTS * 2048 * 2 + 2 * H * 2048 * 2),
        name=f"partial{chunk}",
    )(where, weighted, *buffers)


def grads_kernel(where_ref, factor_ref, gate_ref, up_ref, weight_ref, effective_ref, *refs):
    buffers = refs[: 8 * CHUNKS]
    gate_out, up_out, score_out, rows, eff, turned, total, sems = refs[8 * CHUNKS :]
    step = pl.program_id(0)
    slot = step & 1
    e = step // 4
    part = step & 3

    def copies(at_e, i, into):
        group, chunk = i // 2, i % 2
        quarter = where_ref[8 + group] * 2 + chunk
        return row_copies(
            where_ref, buffers[8 * chunk : 8 * chunk + 8], group, at_e, rows.at[into], sems.at[into]
        ) + [
            pltpu.make_async_copy(
                effective_ref.at[j, quarter, at_e],
                eff.at[into, :, pl.ds(j * UNIT, UNIT)],
                sems.at[into, 4 + j],
            )
            for j in range(NDP)
        ]

    def fetch(at, into):
        for i in range(4):
            @pl.when((at & 3) == i)
            def _(i=i):
                for copy in copies(at // 4, i, into):
                    copy.start()

    @pl.when(step == 0)
    def _():
        fetch(step, 0)

    @pl.when(step < 7)
    def _():
        fetch(step + 1, 1 - slot)

    for copy in copies(0, 0, slot):
        copy.wait()

    half = where_ref[8 + part // 2]
    first = (part & 1) == 0

    def add(target):
        for n in range(H // 256):
            value = lax.dot_general(
                rows[slot],
                eff[slot, n * 256 : (n + 1) * 256, :],
                (((1,), (1,)), ((), ())),
                preferred_element_type=jnp.float32,
            )
            columns = slice(n * 256, (n + 1) * 256)

            @pl.when(first)
            def _(value=value, columns=columns):
                target[:, columns] = value

            @pl.when(jnp.logical_not(first))
            def _(value=value, columns=columns):
                target[:, columns] += value

    @pl.when(half == 0)
    def _():
        add(turned)

    @pl.when(half == 1)
    def _():
        add(total)

    @pl.when(part == 3)
    def _():
        factor = factor_ref[e]

        def piece(i, carry):
            at = pl.ds(pl.multiple_of(i * 2 * PART, 2 * PART), 2 * PART)
            zz = i // 2
            xx = (i - zz * 2) * 2
            one = pl.ds(pl.multiple_of((xx * NZ + zz) * PART, PART), PART)
            two = pl.ds(pl.multiple_of(((xx + 1) * NZ + zz) * PART, PART), PART)
            slot_grads = factor * (
                total[at, :] + jnp.concatenate([turned[one, :], turned[two, :]], axis=0)
            )
            gate = gate_ref[0, at, :].astype(jnp.float32)
            up = up_ref[0, at, :].astype(jnp.float32)
            sig = 1.0 / (1.0 + jnp.exp(-gate))
            activated = gate * sig
            score_out[0, at, :] = jnp.sum(slot_grads * (activated * up), axis=1, keepdims=True)
            scaled = weight_ref[0, at, :] * slot_grads
            gate_out[0, at, :] = (scaled * up * sig * (1.0 + gate * (1.0 - sig))).astype(
                jnp.bfloat16
            )
            up_out[0, at, :] = (scaled * activated).astype(jnp.bfloat16)
            return carry

        lax.fori_loop(0, SLOTS // (2 * PART), piece, 0)


def grads(where, factor, gate, up, slot_weight, effective, buffers):
    any_spec = pl.BlockSpec(memory_space=pl.ANY)
    whole = pl.BlockSpec((1, SLOTS, H), lambda n, s, f: (n // 4, 0, 0))
    column = pl.BlockSpec((1, SLOTS, 1), lambda n, s, f: (n // 4, 0, 0))
    return pl.pallas_call(
        grads_kernel,
        grid_spec=pltpu.PrefetchScalarGridSpec(
            num_scalar_prefetch=2,
            grid=(8,),
            in_specs=[whole, whole, column, any_spec] + [any_spec] * (8 * CHUNKS),
            out_specs=[whole, whole, column],
            scratch_shapes=[
                pltpu.VMEM((2, SLOTS, 1024), jnp.bfloat16),
                pltpu.VMEM((2, H, 1024), jnp.bfloat16),
                pltpu.VMEM((SLOTS, H), jnp.float32),
                pltpu.VMEM((SLOTS, H), jnp.float32),
                pltpu.SemaphoreType.DMA((2, 8)),
            ],
        ),
        out_shape=[
            jax.ShapeDtypeStruct((2, SLOTS, H), jnp.bfloat16),
            jax.ShapeDtypeStruct((2, SLOTS, H), jnp.bfloat16),
            jax.ShapeDtypeStruct((2, SLOTS, 1), jnp.float32),
        ],
        compiler_params=params(),
        cost_estimate=cost(2 * 2 * SLOTS * H * D, 2 * SLOTS * D * 2 + 2 * H * D * 2, 2 * SLOTS * H),
        name="grads",
    )(where, factor, gate, up, slot_weight, effective, *buffers)


def on_device(grad_out, expert_ids, route_weights, gate_values, up_values, w_down):
    me = lax.axis_index("expert")
    core = me % 2
    x = (me // 2) % NX
    z = me // (2 * NX)
    move = lambda value, *to: lax.ppermute(value, "expert", pairs(*to))

    halves = grad_out.reshape(TOK, NDP, 2, CHUNKS, UNIT).transpose(2, 3, 0, 1, 4)
    halves = halves.reshape(2, CHUNKS, TOK, 1024)
    mine = lax.dynamic_index_in_dim(halves, core, 0, keepdims=False)
    theirs = lax.dynamic_index_in_dim(halves, 1 - core, 0, keepdims=False)
    partner = move(theirs, True, 0, 1)
    block = jnp.where(
        core == 0, jnp.stack([mine, partner], axis=1), jnp.stack([partner, mine], axis=1)
    ).reshape(CHUNKS, 2 * TOK, 1024)
    blocks = [block] + [move(block, True, shift, 0) for shift in SHIFTS[1:]]

    shrunk, sums = shrink(w_down)
    effective = lax.all_gather(shrunk, "dp", axis=0)
    sums = lax.psum(jnp.sum(sums, axis=(0, 3, 4)), "dp")
    factor = sums[:, 0] / (sums[:, 1] + epsilon)

    table, rank = route(expert_ids, route_weights)
    tables = lax.all_gather(table, "expert", axis=0)
    slot_weight = lax.dynamic_slice_in_dim(tables[:, :, TOK : TOK + CAP], 2 * me, 2, 1)
    slot_weight = slot_weight.astype(jnp.float32).transpose(1, 0, 2).reshape(2, SLOTS, 1)

    ranks = tables[:, :, :TOK].reshape(NZ, NX, 2, 64, TOK)
    ranks = jnp.where(
        core == 0,
        lax.dynamic_index_in_dim(ranks, x, 1, keepdims=False),
        lax.dynamic_index_in_dim(ranks, z, 0, keepdims=False),
    ).reshape(4, 2, NZ, NX, 2, 2, TOK)
    ranks = jnp.where(
        core == 0,
        lax.dynamic_index_in_dim(ranks, z, 2, keepdims=False),
        lax.dynamic_index_in_dim(ranks, x, 3, keepdims=False),
    )
    place = jnp.where(core == 0, x, z)
    ranks = jnp.stack(
        [
            lax.dynamic_index_in_dim(ranks, (place + shift) % 4, 2, keepdims=False)
            for shift in SHIFTS
        ],
        axis=2,
    )
    ranks = jnp.where(core == 0, ranks, ranks[:, :, :, ::-1])
    ranks = ranks.transpose(0, 2, 3, 4, 1, 5).reshape(4, 16, 2 * TOK).astype(jnp.float32)

    shifts = jnp.array(SHIFTS, jnp.int32)
    held = jnp.where(core == 0, z, x)
    held = ((held - shifts) % 4).astype(jnp.int32)

    gate, up = gate_values[0], up_values[0]
    weighted = weigh(gate, up, slot_weight)

    same = (jnp.where(core == 0, x, z) - shifts) % 4
    other = (jnp.where(core == 0, z, x) - shifts) % 4
    where = jnp.concatenate([same, other, jnp.stack([core, 1 - core])]).astype(jnp.int32)

    buffers, summed = [], []
    for chunk in range(CHUNKS):
        rows = pick(chunk, held, ranks, blocks)
        got = [
            rows[2 * i + swap]
            if i == 0 and swap == 0
            else move(rows[2 * i + swap], False, shift, swap)
            for swap in range(2)
            for i, shift in enumerate(SHIFTS)
        ]
        buffers += got
        part = partial(chunk, where, weighted, got)
        summed.append(lax.psum_scatter(part, "dp", scatter_dimension=0, tiled=False))

    grad_gate, grad_up, scores = grads(where, factor, gate, up, slot_weight, effective, buffers)
    returned = lax.all_to_all(
        scores.reshape(2, SLOTS), "expert", split_axis=1, concat_axis=0, tiled=True
    )
    grad_route = back(expert_ids, rank, returned)

    summed = jnp.stack(summed, axis=1)
    summed = summed.transpose(2, 3, 0, 1, 4).reshape(2, H, 1024)
    grad_down = (factor[:, None, None] * summed.astype(jnp.float32)).astype(jnp.bfloat16)
    return (grad_gate[None], grad_up[None], grad_down, grad_route)


def solution(mesh):
    in_specs = (
        P(("dp", "expert"), None),
        P(("dp", "expert"), None),
        P(("dp", "expert"), None),
        P("dp", "expert", None, None),
        P("dp", "expert", None, None),
        P("expert", None, "dp"),
    )
    out_specs = (
        P("dp", "expert", None, None),
        P("dp", "expert", None, None),
        P("expert", None, "dp"),
        P(("dp", "expert"), None),
    )
    return jax.shard_map(
        on_device, mesh=mesh, in_specs=in_specs, out_specs=out_specs, check_vma=False
    )
```

```python
import functools

import jax
import jax.numpy as jnp
from jax import lax
from jax.experimental import pallas as pl
from jax.experimental.pallas import tpu as pltpu
from jax.sharding import PartitionSpec as P

epsilon = 1e-06

D = 4096
H = 768
TOP = 8
TOK = 256
CAP = 36
SLOTS = 1152
NZ = NX = 4
NDP = 4
PART = 2 * CAP
SEG = NZ * PART
UNIT = 256
HALF = 2 * UNIT
WIDE = NDP * HALF
SHIFTS = (0, 1, 3, 2)
VMEM_LIMIT = 56 * 1024 * 1024


def member(z, x, core):
    return ((z % NZ) * NX + (x % NX)) * 2 + core


def pairs(first_axis, shift, swap):
    out = []
    for z in range(NZ):
        for x in range(NX):
            for core in range(2):
                along_z = (core == 0) == first_axis
                to = (z + shift, x) if along_z else (z, x + shift)
                out.append((member(z, x, core), member(*to, core ^ swap)))
    return out


def params(**kw):
    return pltpu.CompilerParams(vmem_limit_bytes=VMEM_LIMIT, **kw)


def cost(flops, nbytes, trans=0):
    return pl.CostEstimate(flops=int(flops), bytes_accessed=int(nbytes), transcendentals=int(trans))


def shrink_kernel(half_ref, w_ref, out_ref, sums_ref):
    dense = w_ref[0].astype(jnp.float32).reshape(H // 8, 8, UNIT)
    row = lax.broadcasted_iota(jnp.int32, dense.shape, 1)
    odd = (row & 1) == 1
    high = (row & 2) == 2

    def across(value, step, upper):
        return jnp.where(upper, pltpu.roll(value, step, 1), pltpu.roll(value, 8 - step, 1))

    mag = jnp.abs(dense)
    other = across(mag, 1, odd)
    low, up = jnp.minimum(mag, other), jnp.maximum(mag, other)
    second = jnp.minimum(
        jnp.maximum(low, across(low, 2, high)), jnp.minimum(up, across(up, 2, high))
    )
    kept = jnp.maximum(mag - second, 0.0)
    shrunk = jnp.where(dense < 0.0, -kept, kept)
    out_ref[...] = shrunk.reshape(out_ref.shape).astype(jnp.bfloat16)

    def fold(value):
        value = jnp.sum(value, axis=0)
        return value[:, :128] + value[:, 128:]

    sums_ref[0, 0, 0] = fold(dense * shrunk)
    sums_ref[0, 0, 1] = fold(shrunk * shrunk)


def shrink(half, wide, w_down):
    if wide:
        spec = pl.BlockSpec((1, 1, H, UNIT), lambda e, t, s: (1, e, 0, t))
        shape = jax.ShapeDtypeStruct((2, 2, H, HALF), jnp.bfloat16)
    else:
        spec = pl.BlockSpec((1, H, UNIT), lambda e, t, s: (e, 0, t))
        shape = jax.ShapeDtypeStruct((2, H, HALF), jnp.bfloat16)
    return pl.pallas_call(
        shrink_kernel,
        grid_spec=pltpu.PrefetchScalarGridSpec(
            num_scalar_prefetch=1,
            grid=(2, 2),
            in_specs=[pl.BlockSpec((1, H, UNIT), lambda e, t, s: (e, 0, 2 * s[0] + t))],
            out_specs=[spec, pl.BlockSpec((1, 1, 2, 8, 128), lambda e, t, s: (t, e, 0, 0, 0))],
        ),
        out_shape=[shape, jax.ShapeDtypeStruct((2, 2, 2, 8, 128), jnp.float32)],
        compiler_params=params(),
        cost_estimate=cost(2 * H * HALF * 30, 2 * 2 * H * HALF * 2),
        name="shrink",
    )(half.reshape(1).astype(jnp.int32), w_down)


def back_kernel(ids_ref, rank_ref, score_ref, out_ref):
    expert = lax.broadcasted_iota(jnp.int32, (64, TOK), 0)
    rank = rank_ref[...]
    score = jnp.zeros((64, TOK), jnp.float32)
    for slot in range(CAP):
        score = jnp.where(rank == float(slot), score_ref[:, slot : slot + 1], score)
    for k in range(TOP):
        hit = ids_ref[k : k + 1, :] == expert
        out_ref[k : k + 1, :] = jnp.sum(jnp.where(hit, score, 0.0), axis=0, keepdims=True)


def back(ids, rank, score):
    out = pl.pallas_call(
        back_kernel,
        out_shape=jax.ShapeDtypeStruct((TOP, TOK), jnp.float32),
        compiler_params=params(),
        name="back",
    )(ids.T, rank, score)
    return out.T


def split_kernel(core_ref, rows_ref, ids_ref, weights_ref, mine_ref, theirs_ref, share_ref, rank_ref):
    core = core_ref[0]
    owner = pl.program_id(0)

    @pl.when(owner == 0)
    def _():
        expert = lax.broadcasted_iota(jnp.int32, (64, TOK), 0)
        named = jnp.zeros((64, TOK), jnp.float32)
        weight = jnp.zeros((64, TOK), jnp.float32)
        for k in range(TOP):
            hit = ids_ref[k : k + 1, :] == expert
            named = jnp.where(hit, 1.0, named)
            weight = jnp.where(hit, weights_ref[k : k + 1, :], weight)
        earlier = lax.broadcasted_iota(jnp.int32, (TOK, TOK), 0) < lax.broadcasted_iota(
            jnp.int32, (TOK, TOK), 1
        )
        rank = jnp.dot(
            named.astype(jnp.bfloat16),
            jnp.where(earlier, 1.0, 0.0).astype(jnp.bfloat16),
            preferred_element_type=jnp.float32,
        )
        rank = jnp.where(named > 0.0, rank, -1.0)
        rank_ref[...] = rank
        lane = lax.broadcasted_iota(jnp.int32, (64, 128), 1)
        share = jnp.zeros((64, 128), jnp.float32)
        for slot in range(CAP):
            one = jnp.sum(jnp.where(rank == float(slot), weight, 0.0), axis=1, keepdims=True)
            share = jnp.where(lane == slot, one, share)
        share_ref[...] = share.astype(jnp.bfloat16)

    ranks = rank_ref[pl.ds(pl.multiple_of(owner * 16, 16), 16), :].astype(jnp.bfloat16)
    ranks = jnp.concatenate([ranks, jnp.zeros_like(ranks)], axis=1)
    columns = lambda half: pl.ds(pl.multiple_of(half * HALF, HALF), HALF)
    mine_ref[0, :TOK, :] = rows_ref[:, columns(core)]
    theirs_ref[:TOK, :] = rows_ref[:, columns(1 - core)]
    mine_ref[0, TOK:, :] = ranks
    theirs_ref[TOK:, :] = ranks


def split(core, rows, ids, weights):
    deep = TOK + 16
    small = pl.BlockSpec((TOP, TOK), lambda j, s: (0, 0))
    return pl.pallas_call(
        split_kernel,
        grid_spec=pltpu.PrefetchScalarGridSpec(
            num_scalar_prefetch=1,
            grid=(NDP,),
            in_specs=[pl.BlockSpec((TOK, 1024), lambda j, s: (0, j)), small, small],
            out_specs=[
                pl.BlockSpec((1, deep, HALF), lambda j, s: (s[0], 0, j)),
                pl.BlockSpec((deep, HALF), lambda j, s: (0, j)),
                pl.BlockSpec((64, 128), lambda j, s: (0, 0)),
                pl.BlockSpec((64, TOK), lambda j, s: (0, 0)),
            ],
        ),
        out_shape=[
            jax.ShapeDtypeStruct((2, deep, WIDE), jnp.bfloat16),
            jax.ShapeDtypeStruct((deep, WIDE), jnp.bfloat16),
            jax.ShapeDtypeStruct((64, 128), jnp.bfloat16),
            jax.ShapeDtypeStruct((64, TOK), jnp.float32),
        ],
        compiler_params=params(),
        name="split",
    )(core.reshape(1).astype(jnp.int32), rows, ids.T, weights.astype(jnp.float32).T)


def pick_kernel(swap, e, where_ref, *refs):
    outs = refs[5:9]
    tokens, coded, ranks, onehot, picked, sems = refs[9:]
    blocks = [[ref.at[part] for part in range(2)] for ref in refs[:3]] + [refs[3:5]]
    step = pl.program_id(0)
    core = where_ref[8]

    def tile(n):
        columns = pl.ds(pl.multiple_of(n * HALF, HALF), HALF)
        return [
            pltpu.make_async_copy(
                blocks[i][part].at[pl.ds(0, TOK), columns],
                tokens.at[n, where_ref[i], pl.ds(part * TOK, TOK)],
                sems.at[n, 2 * i + part],
            )
            for i in range(4)
            for part in range(2)
        ]

    @pl.when(step == 0)
    def _():
        plane = [jnp.where(core == 0, where_ref[9], where_ref[4 + i]) for i in range(4)]
        inside = [jnp.where(core == 0, where_ref[4 + i], where_ref[9]) for i in range(4)]
        tables = [
            pltpu.make_async_copy(
                blocks[i][part].at[pl.ds(TOK, 16)], coded.at[where_ref[i], part], sems.at[4, 2 * i + part]
            )
            for i in range(4)
            for part in range(2)
        ]
        for copy in tables:
            copy.start()
        for n in range(4):
            for copy in tile(n):
                copy.start()
        for copy in tables:
            copy.wait()
        for block in range(4):
            for part in range(2):
                ranks[block, part] = coded[block, part].astype(jnp.float32)
        row = lax.broadcasted_iota(jnp.int32, (PART, 2 * TOK), 0)
        lane = lax.broadcasted_iota(jnp.int32, (PART, 2 * TOK), 1)
        second = row >= CAP
        slot = jnp.where(second, row - CAP, row)
        slot = jnp.where(second == (lane >= TOK), slot, -2).astype(jnp.float32)
        for i in range(4):
            at = inside[i] * 4 + jnp.where(core == swap, 0, 2) + e
            columns = pl.ds(pl.multiple_of(plane[i] * HALF, HALF), TOK)
            for block in range(4):
                rank = jnp.concatenate(
                    [ranks[block, part, pl.ds(at, 1), columns] for part in range(2)], axis=1
                )
                onehot[block, i * PART : (i + 1) * PART, :] = jnp.where(
                    slot == rank, 1.0, 0.0
                ).astype(jnp.bfloat16)

    for copy in tile(step):
        copy.wait()
    for block in range(4):
        picked[block] = jnp.dot(
            onehot[block], tokens[step, block], preferred_element_type=jnp.float32
        )
    for i in range(4):
        rows = pl.ds(i * PART, PART)
        joined = jnp.concatenate([picked[block, rows, :] for block in range(4)], axis=0)
        outs[i][...] = joined.astype(jnp.bfloat16)


def pick(swap, e, where, blocks):
    any_spec = pl.BlockSpec(memory_space=pl.ANY)
    return pl.pallas_call(
        functools.partial(pick_kernel, swap, e),
        grid_spec=pltpu.PrefetchScalarGridSpec(
            num_scalar_prefetch=1,
            grid=(4,),
            in_specs=[any_spec] * 5,
            out_specs=[pl.BlockSpec((SEG, HALF), lambda n, s: (0, n))] * 4,
            scratch_shapes=[
                pltpu.VMEM((4, 4, 2 * TOK, HALF), jnp.bfloat16),
                pltpu.VMEM((4, 2, 16, WIDE), jnp.bfloat16),
                pltpu.VMEM((4, 2, 16, WIDE), jnp.float32),
                pltpu.VMEM((4, 4 * PART, 2 * TOK), jnp.bfloat16),
                pltpu.VMEM((4, 4 * PART, HALF), jnp.float32),
                pltpu.SemaphoreType.DMA((5, 8)),
            ],
        ),
        out_shape=[jax.ShapeDtypeStruct((SEG, WIDE), jnp.bfloat16)] * 4,
        compiler_params=params(),
        cost_estimate=cost(2 * 4 * 288 * 512 * WIDE, 8 * TOK * WIDE * 2 + 4 * SEG * WIDE * 2),
        name=f"pick{2 * (1 - swap) + e}",
    )(where, *blocks)


def weigh_kernel(core_ref, gate_ref, up_ref, weight_ref, mine_ref, theirs_ref):
    gate = gate_ref[0].astype(jnp.float32)
    up = up_ref[0].astype(jnp.float32)
    sig = 0.5 * jnp.tanh(0.5 * gate) + 0.5
    value = weight_ref[0] * (gate * sig * up)
    turned = jnp.concatenate(
        [
            value[(z * NX + x) * PART : (z * NX + x + 1) * PART]
            for x in range(NX)
            for z in range(NZ)
        ],
        axis=0,
    )
    plain, turned = value.astype(jnp.bfloat16).T, turned.astype(jnp.bfloat16).T

    @pl.when(core_ref[0] == 0)
    def _():
        mine_ref[0] = turned
        theirs_ref[0] = plain

    @pl.when(core_ref[0] == 1)
    def _():
        mine_ref[0] = plain
        theirs_ref[0] = turned


def weigh(core, gate, up, slot_weight):
    wide = 256
    column = pl.BlockSpec((1, SLOTS, wide), lambda e, n, s: (e, 0, n))
    out = pl.BlockSpec((1, wide, SLOTS), lambda e, n, s: (e, n, 0))
    return pl.pallas_call(
        weigh_kernel,
        grid_spec=pltpu.PrefetchScalarGridSpec(
            num_scalar_prefetch=1,
            grid=(2, H // wide),
            in_specs=[column, column, pl.BlockSpec((1, SLOTS, 1), lambda e, n, s: (e, 0, 0))],
            out_specs=[out, out],
        ),
        out_shape=[jax.ShapeDtypeStruct((2, H, SLOTS), jnp.bfloat16)] * 2,
        compiler_params=params(),
        cost_estimate=cost(2 * SLOTS * H * 20, 2 * SLOTS * H * 8, 2 * SLOTS * H),
        name="weigh",
    )(core.reshape(1).astype(jnp.int32), gate, up, slot_weight)


OWNERS = (0, 1, 3, 2)
DEPTH = 3


def segment(where_ref, i):
    return pl.ds(pl.multiple_of(where_ref[i] * SEG, SEG), SEG)


def partial_kernel(experts, ring, where_ref, weighted_ref, *refs):
    count = len(experts)
    buffers = refs[: 4 * count]
    outs, (weights, rows, ready, weight_sems, in_sems, out_sems) = refs[4 * count : -6], refs[-6:]
    steps = [(i, j) for i in range(count) for j in (3, 1, 2, 0)]

    def load(s):
        i, j = steps[s]
        at = lax.rem(where_ref[5] + OWNERS[j], NDP)
        columns = pl.ds(pl.multiple_of(at * HALF, HALF), HALF)
        return [
            pltpu.make_async_copy(
                buffers[4 * i + r].at[:, columns],
                rows.at[s % DEPTH, segment(where_ref, r)],
                in_sems.at[s % DEPTH, r],
            )
            for r in range(4)
        ]

    def store(s):
        i, j = steps[s]
        own, up_first, down_first, up_last, down_last = outs if ring else outs + outs[-1:]
        to = {
            0: [own.at[0, i], own.at[1, i]],
            1: [up_last.at[i], up_first.at[1, i]],
            2: [down_first.at[0, i], down_last.at[i]],
            3: [up_first.at[0, i], down_first.at[1, i]],
        }[j]
        if not ring:
            to = [outs[j].at[p, i] for p in range(2)]
        return [
            pltpu.make_async_copy(ready.at[s % 2, p], to[p], out_sems.at[s % 2, p]) for p in range(2)
        ]

    fetch = [
        pltpu.make_async_copy(weighted_ref.at[e], weights.at[i], weight_sems.at[i])
        for i, e in enumerate(experts)
    ]
    fetch[0].start()
    for s in range(DEPTH):
        for copy in load(s):
            copy.start()
    for copy in fetch[1:]:
        copy.start()
    for s in range(len(steps)):
        i, j = steps[s]
        if s % NDP == 0:
            fetch[i].wait()
        for copy in load(s):
            copy.wait()
        if s >= 2:
            for copy in store(s - 2):
                copy.wait()
        for p in range(2):
            ready[s % 2, p] = jnp.dot(
                weights[i],
                rows[s % DEPTH, :, p * UNIT : (p + 1) * UNIT],
                preferred_element_type=jnp.float32,
            ).astype(jnp.bfloat16)
        for copy in store(s):
            copy.start()
        if s + DEPTH < len(steps):
            for copy in load(s + DEPTH):
                copy.start()
    for s in range(len(steps) - 2, len(steps)):
        for copy in store(s):
            copy.wait()


def partial(experts, ring, where, weighted, buffers):
    any_spec = pl.BlockSpec(memory_space=pl.ANY)
    count = len(experts)
    if ring:
        shapes = [(2, count, H, UNIT)] * 3 + [(count, H, UNIT)] * 2
    else:
        shapes = [(2, count, H, UNIT)] * 4
    return pl.pallas_call(
        functools.partial(partial_kernel, experts, ring),
        grid_spec=pltpu.PrefetchScalarGridSpec(
            num_scalar_prefetch=1,
            grid=(1,),
            in_specs=[any_spec] * (1 + len(buffers)),
            out_specs=[any_spec] * len(shapes),
            scratch_shapes=[
                pltpu.VMEM((count, H, SLOTS), jnp.bfloat16),
                pltpu.VMEM((DEPTH, SLOTS, HALF), jnp.bfloat16),
                pltpu.VMEM((2, 2, H, UNIT), jnp.bfloat16),
                pltpu.SemaphoreType.DMA((count,)),
                pltpu.SemaphoreType.DMA((DEPTH, 4)),
                pltpu.SemaphoreType.DMA((2, 2)),
            ],
        ),
        out_shape=[jax.ShapeDtypeStruct(shape, jnp.bfloat16) for shape in shapes],
        compiler_params=params(),
        cost_estimate=cost(
            count * 2 * SLOTS * H * WIDE, count * (SLOTS * WIDE * 2 + H * WIDE * 2 + H * SLOTS * 2)
        ),
        name="partial",
    )(where, weighted, *buffers)


def grads_kernel(group, e, where_ref, factor_ref, effective_ref, *refs):
    buffers, refs = refs[:4], refs[4:]
    rows, eff, total, sems = refs[-4:]

    def load(k):
        return [
            pltpu.make_async_copy(
                buffers[r].at[:, pl.ds(k * 1024, 1024)],
                rows.at[k, segment(where_ref, r)],
                sems.at[k, r],
            )
            for r in range(4)
        ] + [
            pltpu.make_async_copy(
                effective_ref.at[2 * k + j, group, e],
                eff.at[k, :, pl.ds(j * HALF, HALF)],
                sems.at[k, 4 + j],
            )
            for j in range(2)
        ]

    for k in range(2):
        for copy in load(k):
            copy.start()
    if group:
        before_hbm, gate_hbm, up_hbm, weight_ref = refs[:4]
        gate_out, up_out, score_out, before_ref, gate_ref, up_ref, more_sems = refs[-11:-4]
        more = [
            pltpu.make_async_copy(before_hbm, before_ref, more_sems.at[0]),
            pltpu.make_async_copy(gate_hbm.at[e], gate_ref, more_sems.at[1]),
            pltpu.make_async_copy(up_hbm.at[e], up_ref, more_sems.at[2]),
        ]
        for copy in more:
            copy.start()
    for k in range(2):
        for copy in load(k):
            copy.wait()
        for n in range(H // 256):
            columns = slice(n * 256, (n + 1) * 256)
            value = lax.dot_general(
                rows[k], eff[k, columns, :], (((1,), (1,)), ((), ())), preferred_element_type=jnp.float32
            )
            if k == 0:
                total[:, columns] = value
            else:
                total[:, columns] += value
    if group:
        for copy in more:
            copy.wait()

    def piece(i, carry):
        at = pl.ds(pl.multiple_of(i * 2 * PART, 2 * PART), 2 * PART)
        z = i // 2
        x = (i - z * 2) * 2
        source = [jnp.where(where_ref[4] == 0, (x + k) * NZ + z, 2 * i + k) for k in range(2)]
        product = jnp.concatenate(
            [total[pl.ds(pl.multiple_of(one * PART, PART), PART), :] for one in source], axis=0
        )
        if not group:
            refs[0][at, :] = product
            return carry
        slot_grads = factor_ref[e] * (before_ref[at, :] + product)
        gate = gate_ref[at, :].astype(jnp.float32)
        up = up_ref[at, :].astype(jnp.float32)
        sig = 0.5 * jnp.tanh(0.5 * gate) + 0.5
        activated = gate * sig
        score_out[at, :] = jnp.sum(slot_grads * (activated * up), axis=1, keepdims=True)
        scaled = weight_ref[0, at, :] * slot_grads
        gate_out[0, at, :] = (scaled * up * sig * (1.0 + gate * (1.0 - sig))).astype(jnp.bfloat16)
        up_out[0, at, :] = (scaled * activated).astype(jnp.bfloat16)
        return carry

    lax.fori_loop(0, SLOTS // (2 * PART), piece, 0)


def grads(group, e, where, factor, effective, buffers, others=(), written=()):
    any_spec = pl.BlockSpec(memory_space=pl.ANY)
    scratch = [
        pltpu.VMEM((2, SLOTS, 1024), jnp.bfloat16),
        pltpu.VMEM((2, H, 1024), jnp.bfloat16),
        pltpu.VMEM((SLOTS, H), jnp.float32),
        pltpu.SemaphoreType.DMA((2, 6)),
    ]
    ins = [any_spec] * 5
    if group:
        block = pl.BlockSpec((1, SLOTS, H), lambda n, s, f: (e, 0, 0))
        ins += [any_spec] * 3 + [pl.BlockSpec((1, SLOTS, 1), lambda n, s, f: (e, 0, 0))]
        ins += [any_spec] * len(written)
        outs = [block, block, pl.BlockSpec((SLOTS, 1), lambda n, s, f: (0, 0))]
        shapes = [jax.ShapeDtypeStruct((2, SLOTS, H), jnp.bfloat16)] * 2
        shapes += [jax.ShapeDtypeStruct((SLOTS, 1), jnp.float32)]
        scratch = [
            pltpu.VMEM((SLOTS, H), jnp.float32),
            pltpu.VMEM((SLOTS, H), jnp.bfloat16),
            pltpu.VMEM((SLOTS, H), jnp.bfloat16),
            pltpu.SemaphoreType.DMA((3,)),
        ] + scratch
    else:
        outs = [pl.BlockSpec((SLOTS, H), lambda n, s, f: (0, 0))]
        shapes = [jax.ShapeDtypeStruct((SLOTS, H), jnp.float32)]
    return pl.pallas_call(
        functools.partial(grads_kernel, group, e),
        grid_spec=pltpu.PrefetchScalarGridSpec(
            num_scalar_prefetch=2, grid=(1,), in_specs=ins, out_specs=outs, scratch_shapes=scratch
        ),
        out_shape=shapes,
        input_output_aliases={11 + i: i for i in range(len(written))},
        compiler_params=params(),
        cost_estimate=cost(
            2 * SLOTS * H * WIDE + group * SLOTS * H * 30,
            SLOTS * WIDE * 2 + H * WIDE * 2 + SLOTS * H * (12 if group else 4),
        ),
        name=f"grads{2 * group + e}",
    )(where, factor, effective, *buffers, *others, *written)


def finish_kernel(where_ref, factor_ref, theirs, *refs):
    first, second, out_ref = refs[:5], refs[5:9], refs[9]
    wide = lambda value: value.astype(jnp.float32)
    e = pl.program_id(0)
    factor = factor_ref[e]
    mine = [pl.ds(pl.multiple_of(where_ref[4] * HALF + p * UNIT, UNIT), UNIT) for p in range(2)]
    for p in range(2):
        other = pl.ds(pl.multiple_of((1 - where_ref[4]) * HALF + p * UNIT, UNIT), UNIT)
        out_ref[0, :, other] = (factor * wide(theirs[p, 0])).astype(jnp.bfloat16)

    @pl.when(e == 0)
    def _():
        own, up, down, low, high = first
        sums = (
            wide(own[0, 0]) + (wide(low[0]) + wide(down[0, 0])),
            wide(own[1, 0]) + (wide(up[1, 0]) + wide(high[0])),
        )
        for p in range(2):
            out_ref[0, :, mine[p]] = (factor * sums[p]).astype(jnp.bfloat16)

    @pl.when(e == 1)
    def _():
        for p in range(2):
            total = (wide(second[0][p, 0]) + wide(second[1][p, 0])) + (
                wide(second[2][p, 0]) + wide(second[3][p, 0])
            )
            out_ref[0, :, mine[p]] = (factor * total).astype(jnp.bfloat16)


def finish(where, factor, theirs, first, second):
    pair = pl.BlockSpec((2, 1, H, UNIT), lambda n, s, f: (0, 0, 0, 0))
    single = pl.BlockSpec((1, H, UNIT), lambda n, s, f: (0, 0, 0))
    return pl.pallas_call(
        finish_kernel,
        grid_spec=pltpu.PrefetchScalarGridSpec(
            num_scalar_prefetch=2,
            grid=(2,),
            in_specs=[pl.BlockSpec((2, 1, H, UNIT), lambda n, s, f: (0, n, 0, 0))]
            + [pair] * 3
            + [single] * 2
            + [pair] * 4,
            out_specs=pl.BlockSpec((1, H, 1024), lambda n, s, f: (n, 0, 0)),
        ),
        out_shape=jax.ShapeDtypeStruct((2, H, 1024), jnp.bfloat16),
        compiler_params=params(),
        name="finish",
    )(where, factor, theirs, *first, *second)


def after(value, *first):
    return lax.optimization_barrier((value, *first))[0]


def on_device(grad_out, expert_ids, route_weights, gate_values, up_values, w_down):
    me = lax.axis_index("expert")
    y = lax.axis_index("dp")
    core = me % 2
    x = (me // 2) % NX
    z = me // (2 * NX)
    move = lambda value, *to: lax.ppermute(value, "expert", pairs(*to))
    swap = lambda value: move(value, True, 0, 1)
    upward = lambda value: lax.ppermute(value, "dp", [(i, (i + 1) % NDP) for i in range(NDP)])
    across = lambda value: lax.ppermute(value, "dp", [(i, (i + 2) % NDP) for i in range(NDP)])
    downward = lambda value: lax.ppermute(value, "dp", [(i, (i - 1) % NDP) for i in range(NDP)])

    mine, theirs, share, rank = split(core, grad_out, expert_ids, route_weights)
    partner = swap(theirs)
    given, given_sums = shrink(1 - core, False, after(w_down, theirs))
    block = lax.dynamic_update_slice(mine, partner[None], (1 - core, 0, 0))
    block = after(block, given)
    blocks = [block, move(block, True, 1, 0), move(block, True, -1, 0)]
    blocks += [move(blocks[1][0], True, 1, 0), move(blocks[2][1], True, -1, 0)]
    kept, kept_sums = shrink(core, True, after(w_down, upward(given_sums)))
    effective = lax.dynamic_update_slice(kept, swap(given)[None], (0, 0, 0, 0))
    effective = lax.all_gather(effective, "dp", axis=0)

    share = share[:, :CAP].reshape(NZ * NX * 2, 2, CAP)
    share = lax.all_to_all(share, "expert", split_axis=0, concat_axis=0, tiled=True)
    sums = jnp.sum(given_sums + kept_sums, axis=(0, 3, 4))
    below, above = upward(sums), downward(sums)
    sums = (sums + upward(below)) + (below + above)
    factor = sums[:, 0] / (sums[:, 1] + epsilon)

    first, second = jnp.where(core == 0, z, x), jnp.where(core == 0, x, z)
    around = lambda value, sign: [(value + sign * shift) % 4 for shift in SHIFTS]
    held = jnp.stack([*around(first, -1), *around(second, 1), core, first]).astype(jnp.int32)
    where = jnp.stack([*around(second, -1), core, y]).astype(jnp.int32)
    gate, up = gate_values[0], up_values[0]

    def send(rows, before):
        return [rows[0]] + [
            move(after(rows[i], *before), False, SHIFTS[i], 0) for i in range(1, 4)
        ]

    rows = pick(1, 0, after(held, factor, share), blocks)
    units = [send(rows, [])]
    rows = pick(1, 1, after(held, *rows), blocks)
    slot_weight = after(share, *rows).astype(jnp.float32).transpose(1, 0, 2).reshape(2, SLOTS, 1)
    weighted, their_weighted = weigh(core, gate, up, slot_weight)
    units.append(send(rows, units[0][1:] + [weighted]))
    rows = pick(0, 0, after(held, weighted), blocks)
    last_rows = pick(0, 1, after(held, *rows), blocks)
    units.append(send(rows, units[1][1:] + list(last_rows)))

    def exchange(pieces):
        own, up_first, down_first, up_last, down_last = pieces
        return own, upward(up_first), downward(down_first), up_last, down_last

    def complete(pieces, *before):
        own, up_first, down_first, up_last, down_last = pieces
        up_last = upward(after(up_last, *before) + up_first[0])
        down_last = downward(after(down_last, *before) + down_first[1])
        return own, up_first, down_first, up_last, down_last

    their_weighted = swap(after(their_weighted, *units[0][1:]))
    theirs = partial((0, 1), True, where, their_weighted, units[0] + units[1])
    before = [grads(0, 0, where, factor, effective, units[0])[0]]
    units.append(send(last_rows, units[2][1:] + list(theirs) + before))
    theirs = exchange(theirs)
    early = partial((0,), True, where, weighted, units[2])
    before += [grads(0, 1, after(where, *early, *theirs[1:3]), factor, effective, units[1])[0]]
    late = partial((1,), False, where, after(weighted, before[1]), units[3])
    early = exchange(early)
    late = [late[0], upward(late[1]), downward(late[2]), across(late[3])]
    before = [swap(after(value, late[0], *early[1:3])) for value in before]
    *written, score0 = grads(
        1, 0, where, factor, effective, units[2], (before[0], gate, up, slot_weight)
    )
    *written, score1 = grads(
        1, 1, where, factor, effective, units[3], (before[1], gate, up, slot_weight), written
    )
    theirs = complete(theirs, score0, score1, *late[1:])
    early = complete(early, score0, score1, *late[1:])
    scores = [score0, score1]
    grad_gate, grad_up = written
    scores = jnp.stack(scores).reshape(2, SLOTS)
    returned = lax.all_to_all(scores, "expert", split_axis=1, concat_axis=0, tiled=True)
    grad_route = back(expert_ids, rank, returned)

    own, up_first, down_first, up_last, down_last = [value.astype(jnp.float32) for value in theirs]
    summed = jnp.stack([own[0] + (up_last + down_first[0]), own[1] + (up_first[1] + down_last)])
    summed = swap(summed.astype(jnp.bfloat16))
    grad_down = finish(where, factor, summed, early, late)
    return (grad_gate[None], grad_up[None], grad_down, grad_route)


def solution(mesh):
    in_specs = (
        P(("dp", "expert"), None),
        P(("dp", "expert"), None),
        P(("dp", "expert"), None),
        P("dp", "expert", None, None),
        P("dp", "expert", None, None),
        P("expert", None, "dp"),
    )
    out_specs = (
        P("dp", "expert", None, None),
        P("dp", "expert", None, None),
        P("expert", None, "dp"),
        P(("dp", "expert"), None),
    )
    return jax.shard_map(
        on_device, mesh=mesh, in_specs=in_specs, out_specs=out_specs, check_vma=False
    )
```

```python
import functools

import jax
import jax.numpy as jnp
from jax import lax
from jax.experimental import pallas as pl
from jax.experimental.pallas import tpu as pltpu
from jax.sharding import PartitionSpec as P

epsilon = 1e-06

D = 4096
H = 768
TOP = 8
TOK = 256
CAP = 36
SLOTS = 1152
NZ = NX = 4
NDP = 4
PART = 2 * CAP
SEG = NZ * PART
UNIT = 256
HALF = 2 * UNIT
WIDE = NDP * HALF
SHIFTS = (0, 1, 3, 2)
VMEM_LIMIT = 56 * 1024 * 1024


def member(z, x, core):
    return ((z % NZ) * NX + (x % NX)) * 2 + core


def pairs(first_axis, shift, swap):
    out = []
    for z in range(NZ):
        for x in range(NX):
            for core in range(2):
                along_z = (core == 0) == first_axis
                to = (z + shift, x) if along_z else (z, x + shift)
                out.append((member(z, x, core), member(*to, core ^ swap)))
    return out


def params(**kw):
    return pltpu.CompilerParams(vmem_limit_bytes=VMEM_LIMIT, **kw)


def cost(flops, nbytes, trans=0):
    return pl.CostEstimate(flops=int(flops), bytes_accessed=int(nbytes), transcendentals=int(trans))


def shrink_kernel(half_ref, w_ref, out_ref, sums_ref):
    dense = w_ref[0].astype(jnp.float32).reshape(H // 8, 8, UNIT)
    row = lax.broadcasted_iota(jnp.int32, dense.shape, 1)
    odd = (row & 1) == 1
    high = (row & 2) == 2

    def across(value, step, upper):
        return jnp.where(upper, pltpu.roll(value, step, 1), pltpu.roll(value, 8 - step, 1))

    mag = jnp.abs(dense)
    other = across(mag, 1, odd)
    low, up = jnp.minimum(mag, other), jnp.maximum(mag, other)
    second = jnp.minimum(
        jnp.maximum(low, across(low, 2, high)), jnp.minimum(up, across(up, 2, high))
    )
    kept = jnp.maximum(mag - second, 0.0)
    shrunk = jnp.where(dense < 0.0, -kept, kept)
    out_ref[...] = shrunk.reshape(out_ref.shape).astype(jnp.bfloat16)

    def fold(value):
        value = jnp.sum(value, axis=0)
        return value[:, :128] + value[:, 128:]

    sums_ref[0, 0, 0] = fold(dense * shrunk)
    sums_ref[0, 0, 1] = fold(shrunk * shrunk)


def shrink(half, wide, w_down):
    if wide:
        spec = pl.BlockSpec((1, 1, H, UNIT), lambda e, t, s: (1, e, 0, t))
        shape = jax.ShapeDtypeStruct((2, 2, H, HALF), jnp.bfloat16)
    else:
        spec = pl.BlockSpec((1, H, UNIT), lambda e, t, s: (e, 0, t))
        shape = jax.ShapeDtypeStruct((2, H, HALF), jnp.bfloat16)
    return pl.pallas_call(
        shrink_kernel,
        grid_spec=pltpu.PrefetchScalarGridSpec(
            num_scalar_prefetch=1,
            grid=(2, 2),
            in_specs=[pl.BlockSpec((1, H, UNIT), lambda e, t, s: (e, 0, 2 * s[0] + t))],
            out_specs=[spec, pl.BlockSpec((1, 1, 2, 8, 128), lambda e, t, s: (t, e, 0, 0, 0))],
        ),
        out_shape=[shape, jax.ShapeDtypeStruct((2, 2, 2, 8, 128), jnp.float32)],
        compiler_params=params(),
        cost_estimate=cost(2 * H * HALF * 30, 2 * 2 * H * HALF * 2),
        name="shrink",
    )(half.reshape(1).astype(jnp.int32), w_down)


def back_kernel(ids_ref, rank_ref, score_ref, out_ref):
    expert = lax.broadcasted_iota(jnp.int32, (64, TOK), 0)
    rank = rank_ref[...]
    score = jnp.zeros((64, TOK), jnp.float32)
    for slot in range(CAP):
        score = jnp.where(rank == float(slot), score_ref[:, slot : slot + 1], score)
    for k in range(TOP):
        hit = ids_ref[k : k + 1, :] == expert
        out_ref[k : k + 1, :] = jnp.sum(jnp.where(hit, score, 0.0), axis=0, keepdims=True)


def back(ids, rank, score):
    out = pl.pallas_call(
        back_kernel,
        out_shape=jax.ShapeDtypeStruct((TOP, TOK), jnp.float32),
        compiler_params=params(),
        name="back",
    )(ids.T, rank, score)
    return out.T


def split_kernel(core_ref, rows_ref, ids_ref, weights_ref, mine_ref, theirs_ref, share_ref, rank_ref):
    core = core_ref[0]
    owner = pl.program_id(0)

    @pl.when(owner == 0)
    def _():
        expert = lax.broadcasted_iota(jnp.int32, (64, TOK), 0)
        named = jnp.zeros((64, TOK), jnp.float32)
        weight = jnp.zeros((64, TOK), jnp.float32)
        for k in range(TOP):
            hit = ids_ref[k : k + 1, :] == expert
            named = jnp.where(hit, 1.0, named)
            weight = jnp.where(hit, weights_ref[k : k + 1, :], weight)
        earlier = lax.broadcasted_iota(jnp.int32, (TOK, TOK), 0) < lax.broadcasted_iota(
            jnp.int32, (TOK, TOK), 1
        )
        rank = jnp.dot(
            named.astype(jnp.bfloat16),
            jnp.where(earlier, 1.0, 0.0).astype(jnp.bfloat16),
            preferred_element_type=jnp.float32,
        )
        rank = jnp.where(named > 0.0, rank, -1.0)
        rank_ref[...] = rank
        lane = lax.broadcasted_iota(jnp.int32, (64, 128), 1)
        share = jnp.zeros((64, 128), jnp.float32)
        for slot in range(CAP):
            one = jnp.sum(jnp.where(rank == float(slot), weight, 0.0), axis=1, keepdims=True)
            share = jnp.where(lane == slot, one, share)
        share_ref[...] = share.astype(jnp.bfloat16)

    ranks = rank_ref[pl.ds(pl.multiple_of(owner * 16, 16), 16), :].astype(jnp.bfloat16)
    ranks = jnp.concatenate([ranks, jnp.zeros_like(ranks)], axis=1)
    columns = lambda half: pl.ds(pl.multiple_of(half * HALF, HALF), HALF)
    mine_ref[0, :TOK, :] = rows_ref[:, columns(core)]
    theirs_ref[:TOK, :] = rows_ref[:, columns(1 - core)]
    mine_ref[0, TOK:, :] = ranks
    theirs_ref[TOK:, :] = ranks


def split(core, rows, ids, weights):
    deep = TOK + 16
    small = pl.BlockSpec((TOP, TOK), lambda j, s: (0, 0))
    return pl.pallas_call(
        split_kernel,
        grid_spec=pltpu.PrefetchScalarGridSpec(
            num_scalar_prefetch=1,
            grid=(NDP,),
            in_specs=[pl.BlockSpec((TOK, 1024), lambda j, s: (0, j)), small, small],
            out_specs=[
                pl.BlockSpec((1, deep, HALF), lambda j, s: (s[0], 0, j)),
                pl.BlockSpec((deep, HALF), lambda j, s: (0, j)),
                pl.BlockSpec((64, 128), lambda j, s: (0, 0)),
                pl.BlockSpec((64, TOK), lambda j, s: (0, 0)),
            ],
        ),
        out_shape=[
            jax.ShapeDtypeStruct((2, deep, WIDE), jnp.bfloat16),
            jax.ShapeDtypeStruct((deep, WIDE), jnp.bfloat16),
            jax.ShapeDtypeStruct((64, 128), jnp.bfloat16),
            jax.ShapeDtypeStruct((64, TOK), jnp.float32),
        ],
        compiler_params=params(),
        name="split",
    )(core.reshape(1).astype(jnp.int32), rows, ids.T, weights.astype(jnp.float32).T)


def pick_kernel(swap, where_ref, *refs):
    outs = refs[5:9]
    tokens, coded, ranks, onehot, picked, sems = refs[9:]
    blocks = [[ref.at[part] for part in range(2)] for ref in refs[:3]] + [refs[3:5]]
    step = pl.program_id(0)
    core = where_ref[8]

    def tile(n):
        columns = pl.ds(pl.multiple_of(n * HALF, HALF), HALF)
        return [
            pltpu.make_async_copy(
                blocks[i][part].at[pl.ds(0, TOK), columns],
                tokens.at[n, where_ref[i], pl.ds(part * TOK, TOK)],
                sems.at[n, 2 * i + part],
            )
            for i in range(4)
            for part in range(2)
        ]

    @pl.when(step == 0)
    def _():
        plane = [jnp.where(core == 0, where_ref[9], where_ref[4 + i]) for i in range(4)]
        inside = [jnp.where(core == 0, where_ref[4 + i], where_ref[9]) for i in range(4)]
        tables = [
            pltpu.make_async_copy(
                blocks[i][part].at[pl.ds(TOK, 16)], coded.at[where_ref[i], part], sems.at[4, 2 * i + part]
            )
            for i in range(4)
            for part in range(2)
        ]
        for copy in tables:
            copy.start()
        for n in range(4):
            for copy in tile(n):
                copy.start()
        for copy in tables:
            copy.wait()
        for block in range(4):
            for part in range(2):
                ranks[block, part] = coded[block, part].astype(jnp.float32)
        row = lax.broadcasted_iota(jnp.int32, (PART, 2 * TOK), 0)
        lane = lax.broadcasted_iota(jnp.int32, (PART, 2 * TOK), 1)
        second = row >= CAP
        slot = jnp.where(second, row - CAP, row)
        slot = jnp.where(second == (lane >= TOK), slot, -2).astype(jnp.float32)
        for i in range(8):
            to, e = i // 2, i % 2
            at = inside[to] * 4 + jnp.where(core == swap, 0, 2) + e
            columns = pl.ds(pl.multiple_of(plane[to] * HALF, HALF), TOK)
            for block in range(4):
                rank = jnp.concatenate(
                    [ranks[block, part, pl.ds(at, 1), columns] for part in range(2)], axis=1
                )
                onehot[block, i * PART : (i + 1) * PART, :] = jnp.where(
                    slot == rank, 1.0, 0.0
                ).astype(jnp.bfloat16)

    for copy in tile(step):
        copy.wait()
    for block in range(4):
        picked[block] = jnp.dot(
            onehot[block], tokens[step, block], preferred_element_type=jnp.float32
        )
    for i in range(8):
        rows = pl.ds(i * PART, PART)
        joined = jnp.concatenate([picked[block, rows, :] for block in range(4)], axis=0)
        outs[i // 2][i % 2] = joined.astype(jnp.bfloat16)


def pick(swap, where, blocks):
    any_spec = pl.BlockSpec(memory_space=pl.ANY)
    return pl.pallas_call(
        functools.partial(pick_kernel, swap),
        grid_spec=pltpu.PrefetchScalarGridSpec(
            num_scalar_prefetch=1,
            grid=(4,),
            in_specs=[any_spec] * 5,
            out_specs=[pl.BlockSpec((2, SEG, HALF), lambda n, s: (0, 0, n))] * 4,
            scratch_shapes=[
                pltpu.VMEM((4, 4, 2 * TOK, HALF), jnp.bfloat16),
                pltpu.VMEM((4, 2, 16, WIDE), jnp.bfloat16),
                pltpu.VMEM((4, 2, 16, WIDE), jnp.float32),
                pltpu.VMEM((4, 8 * PART, 2 * TOK), jnp.bfloat16),
                pltpu.VMEM((4, 8 * PART, HALF), jnp.float32),
                pltpu.SemaphoreType.DMA((5, 8)),
            ],
        ),
        out_shape=[jax.ShapeDtypeStruct((2, SEG, WIDE), jnp.bfloat16)] * 4,
        compiler_params=params(),
        cost_estimate=cost(2 * 4 * 576 * 512 * WIDE, 8 * TOK * WIDE * 2 + 8 * SEG * WIDE * 2),
        name=f"pick{1 - swap}",
    )(where, *blocks)


def weigh_kernel(core_ref, gate_ref, up_ref, weight_ref, mine_ref, theirs_ref):
    gate = gate_ref[0].astype(jnp.float32)
    up = up_ref[0].astype(jnp.float32)
    sig = 0.5 * jnp.tanh(0.5 * gate) + 0.5
    value = weight_ref[0] * (gate * sig * up)
    turned = jnp.concatenate(
        [
            value[(z * NX + x) * PART : (z * NX + x + 1) * PART]
            for x in range(NX)
            for z in range(NZ)
        ],
        axis=0,
    )
    plain, turned = value.astype(jnp.bfloat16).T, turned.astype(jnp.bfloat16).T

    @pl.when(core_ref[0] == 0)
    def _():
        mine_ref[0] = turned
        theirs_ref[0] = plain

    @pl.when(core_ref[0] == 1)
    def _():
        mine_ref[0] = plain
        theirs_ref[0] = turned


def weigh(core, gate, up, slot_weight):
    wide = 256
    column = pl.BlockSpec((1, SLOTS, wide), lambda e, n, s: (e, 0, n))
    out = pl.BlockSpec((1, wide, SLOTS), lambda e, n, s: (e, n, 0))
    return pl.pallas_call(
        weigh_kernel,
        grid_spec=pltpu.PrefetchScalarGridSpec(
            num_scalar_prefetch=1,
            grid=(2, H // wide),
            in_specs=[column, column, pl.BlockSpec((1, SLOTS, 1), lambda e, n, s: (e, 0, 0))],
            out_specs=[out, out],
        ),
        out_shape=[jax.ShapeDtypeStruct((2, H, SLOTS), jnp.bfloat16)] * 2,
        compiler_params=params(),
        cost_estimate=cost(2 * SLOTS * H * 20, 2 * SLOTS * H * 8, 2 * SLOTS * H),
        name="weigh",
    )(core.reshape(1).astype(jnp.int32), gate, up, slot_weight)


OWNERS = (0, 1, 3, 2)
DEPTH = 3


def segment(where_ref, i):
    return pl.ds(pl.multiple_of(where_ref[i] * SEG, SEG), SEG)


def partial_kernel(ring, where_ref, weighted_ref, *refs):
    buffers, outs = refs[:4], refs[4:-6]
    weights, rows, ready, weight_sems, in_sems, out_sems = refs[-6:]
    steps = [(i, j) for i in range(2) for j in (3, 1, 2, 0)]

    def load(s):
        i, j = steps[s]
        at = lax.rem(where_ref[5] + OWNERS[j], NDP) if ring else j
        columns = pl.ds(pl.multiple_of(at * HALF, HALF), HALF)
        return [
            pltpu.make_async_copy(
                buffers[r].at[i, :, columns],
                rows.at[s % DEPTH, segment(where_ref, r)],
                in_sems.at[s % DEPTH, r],
            )
            for r in range(4)
        ]

    def store(s):
        i, j = steps[s]
        if ring:
            own, up_first, down_first, up_last, down_last = outs
            to = {
                0: [own.at[0, i], own.at[1, i]],
                1: [up_last.at[i], up_first.at[1, i]],
                2: [down_first.at[0, i], down_last.at[i]],
                3: [up_first.at[0, i], down_first.at[1, i]],
            }[j]
        else:
            to = [outs[0].at[j, p, i] for p in range(2)]
        return [
            pltpu.make_async_copy(ready.at[s % 2, p], to[p], out_sems.at[s % 2, p]) for p in range(2)
        ]

    fetch = [
        pltpu.make_async_copy(weighted_ref.at[i], weights.at[i], weight_sems.at[i]) for i in range(2)
    ]
    fetch[0].start()
    for s in range(DEPTH):
        for copy in load(s):
            copy.start()
    for copy in fetch[1:]:
        copy.start()
    for s in range(len(steps)):
        i, j = steps[s]
        if s % NDP == 0:
            fetch[i].wait()
        for copy in load(s):
            copy.wait()
        if s >= 2:
            for copy in store(s - 2):
                copy.wait()
        for p in range(2):
            ready[s % 2, p] = jnp.dot(
                weights[i],
                rows[s % DEPTH, :, p * UNIT : (p + 1) * UNIT],
                preferred_element_type=jnp.float32,
            ).astype(jnp.bfloat16)
        for copy in store(s):
            copy.start()
        if s + DEPTH < len(steps):
            for copy in load(s + DEPTH):
                copy.start()
    for s in range(len(steps) - 2, len(steps)):
        for copy in store(s):
            copy.wait()


def partial(ring, where, weighted, buffers):
    any_spec = pl.BlockSpec(memory_space=pl.ANY)
    shapes = [(2, 2, H, UNIT)] * 3 + [(2, H, UNIT)] * 2 if ring else [(NDP, 2, 2, H, UNIT)]
    return pl.pallas_call(
        functools.partial(partial_kernel, ring),
        grid_spec=pltpu.PrefetchScalarGridSpec(
            num_scalar_prefetch=1,
            grid=(1,),
            in_specs=[any_spec] * (1 + len(buffers)),
            out_specs=[any_spec] * len(shapes),
            scratch_shapes=[
                pltpu.VMEM((2, H, SLOTS), jnp.bfloat16),
                pltpu.VMEM((DEPTH, SLOTS, HALF), jnp.bfloat16),
                pltpu.VMEM((2, 2, H, UNIT), jnp.bfloat16),
                pltpu.SemaphoreType.DMA((2,)),
                pltpu.SemaphoreType.DMA((DEPTH, 4)),
                pltpu.SemaphoreType.DMA((2, 2)),
            ],
        ),
        out_shape=[jax.ShapeDtypeStruct(shape, jnp.bfloat16) for shape in shapes],
        compiler_params=params(),
        cost_estimate=cost(
            2 * 2 * SLOTS * H * WIDE, 2 * (SLOTS * WIDE * 2 + H * WIDE * 2 + H * SLOTS * 2)
        ),
        name="partial",
    )(where, weighted, *buffers)


def grads_kernel(group, where_ref, factor_ref, effective_ref, *refs):
    buffers, refs = refs[:4], refs[4:]
    rows, eff, total, sems = refs[-4:]
    e = pl.program_id(0)

    def load(at, k):
        return [
            pltpu.make_async_copy(
                buffers[r].at[at, :, pl.ds(k * 1024, 1024)],
                rows.at[k, segment(where_ref, r)],
                sems.at[k, r],
            )
            for r in range(4)
        ] + [
            pltpu.make_async_copy(
                effective_ref.at[2 * k + j, group, at],
                eff.at[k, :, pl.ds(j * HALF, HALF)],
                sems.at[k, 4 + j],
            )
            for j in range(2)
        ]

    @pl.when(e == 0)
    def _():
        for k in range(2):
            for copy in load(0, k):
                copy.start()

    for k in range(2):
        for copy in load(e, k):
            copy.wait()
        for n in range(H // 256):
            columns = slice(n * 256, (n + 1) * 256)
            value = lax.dot_general(
                rows[k], eff[k, columns, :], (((1,), (1,)), ((), ())), preferred_element_type=jnp.float32
            )
            if k == 0:
                total[:, columns] = value
            else:
                total[:, columns] += value

        @pl.when(e == 0)
        def _(k=k):
            for copy in load(1, k):
                copy.start()

    def piece(i, carry):
        at = pl.ds(pl.multiple_of(i * 2 * PART, 2 * PART), 2 * PART)
        z = i // 2
        x = (i - z * 2) * 2
        source = [jnp.where(where_ref[4] == 0, (x + k) * NZ + z, 2 * i + k) for k in range(2)]
        product = jnp.concatenate(
            [total[pl.ds(pl.multiple_of(one * PART, PART), PART), :] for one in source], axis=0
        )
        if not group:
            refs[0][0, at, :] = product
            return carry
        before_ref, gate_ref, up_ref, weight_ref, gate_out, up_out, score_out = refs[:7]
        slot_grads = factor_ref[e] * (before_ref[0, at, :] + product)
        gate = gate_ref[0, at, :].astype(jnp.float32)
        up = up_ref[0, at, :].astype(jnp.float32)
        sig = 0.5 * jnp.tanh(0.5 * gate) + 0.5
        activated = gate * sig
        score_out[0, at, :] = jnp.sum(slot_grads * (activated * up), axis=1, keepdims=True)
        scaled = weight_ref[0, at, :] * slot_grads
        gate_out[0, at, :] = (scaled * up * (sig + activated * (1.0 - sig))).astype(jnp.bfloat16)
        up_out[0, at, :] = (scaled * activated).astype(jnp.bfloat16)
        return carry

    lax.fori_loop(0, SLOTS // (2 * PART), piece, 0)


def grads(group, where, factor, effective, buffers, others=()):
    any_spec = pl.BlockSpec(memory_space=pl.ANY)
    block = pl.BlockSpec((1, SLOTS, H), lambda n, s, f: (n, 0, 0))
    column = pl.BlockSpec((1, SLOTS, 1), lambda n, s, f: (n, 0, 0))
    shape = lambda dtype, width=H: jax.ShapeDtypeStruct((2, SLOTS, width), dtype)
    if group:
        ins, outs = [block, block, block, column], [block, block, column]
        shapes = [shape(jnp.bfloat16), shape(jnp.bfloat16), shape(jnp.float32, 1)]
    else:
        ins, outs, shapes = [], [block], [shape(jnp.float32)]
    return pl.pallas_call(
        functools.partial(grads_kernel, group),
        grid_spec=pltpu.PrefetchScalarGridSpec(
            num_scalar_prefetch=2,
            grid=(2,),
            in_specs=[any_spec] * 5 + ins,
            out_specs=outs,
            scratch_shapes=[
                pltpu.VMEM((2, SLOTS, 1024), jnp.bfloat16),
                pltpu.VMEM((2, H, 1024), jnp.bfloat16),
                pltpu.VMEM((SLOTS, H), jnp.float32),
                pltpu.SemaphoreType.DMA((2, 6)),
            ],
        ),
        out_shape=shapes,
        compiler_params=params(),
        cost_estimate=cost(
            2 * 2 * SLOTS * H * WIDE + group * 2 * SLOTS * H * 30,
            2 * (SLOTS * WIDE * 2 + H * WIDE * 2 + SLOTS * H * (12 if group else 4)),
        ),
        name=f"grads{group}",
    )(where, factor, effective, *buffers, *others)


def collect(own, up, down, low, high):
    wide = lambda value: value.astype(jnp.float32)
    return (
        wide(own[0, 0]) + (wide(low[0]) + wide(down[0, 0])),
        wide(own[1, 0]) + (wide(up[1, 0]) + wide(high[0])),
    )


PAIR = pl.BlockSpec((2, 1, H, UNIT), lambda n, *s: (0, n, 0, 0))
SINGLE = pl.BlockSpec((1, H, UNIT), lambda n, *s: (n, 0, 0))


def finish_kernel(where_ref, factor_ref, theirs, *refs):
    out_ref = refs[5]
    core = where_ref[4]
    factor = factor_ref[pl.program_id(0)]
    for p, value in enumerate(collect(*refs[:5])):
        mine = pl.ds(pl.multiple_of(core * HALF + p * UNIT, UNIT), UNIT)
        other = pl.ds(pl.multiple_of((1 - core) * HALF + p * UNIT, UNIT), UNIT)
        out_ref[0, :, mine] = (factor * value).astype(jnp.bfloat16)
        out_ref[0, :, other] = (factor * theirs[p, 0].astype(jnp.float32)).astype(jnp.bfloat16)


def finish(where, factor, theirs, pieces):
    return pl.pallas_call(
        finish_kernel,
        grid_spec=pltpu.PrefetchScalarGridSpec(
            num_scalar_prefetch=2,
            grid=(2,),
            in_specs=[PAIR] * 4 + [SINGLE] * 2,
            out_specs=pl.BlockSpec((1, H, 1024), lambda n, *s: (n, 0, 0)),
        ),
        out_shape=jax.ShapeDtypeStruct((2, H, 1024), jnp.bfloat16),
        compiler_params=params(),
        name="finish",
    )(where, factor, theirs, *pieces)


def after(value, *first):
    return lax.optimization_barrier((value, *first))[0]


def on_device(grad_out, expert_ids, route_weights, gate_values, up_values, w_down):
    me = lax.axis_index("expert")
    y = lax.axis_index("dp")
    core = me % 2
    x = (me // 2) % NX
    z = me // (2 * NX)
    move = lambda value, *to: lax.ppermute(value, "expert", pairs(*to))
    swap = lambda value: move(value, True, 0, 1)
    upward = lambda value: lax.ppermute(value, "dp", [(i, (i + 1) % NDP) for i in range(NDP)])
    downward = lambda value: lax.ppermute(value, "dp", [(i, (i - 1) % NDP) for i in range(NDP)])

    mine, theirs, share, rank = split(core, grad_out, expert_ids, route_weights)
    partner = swap(theirs)
    given, given_sums = shrink(1 - core, False, after(w_down, theirs))
    block = lax.dynamic_update_slice(mine, partner[None], (1 - core, 0, 0))
    block = after(block, given)
    blocks = [block, move(block, True, 1, 0), move(block, True, -1, 0)]
    blocks += [move(blocks[1][0], True, 1, 0), move(blocks[2][1], True, -1, 0)]
    kept, kept_sums = shrink(core, True, after(w_down, upward(given_sums)))
    effective = lax.dynamic_update_slice(kept, swap(given)[None], (0, 0, 0, 0))
    effective = lax.all_gather(effective, "dp", axis=0)

    share = share[:, :CAP].reshape(NZ * NX * 2, 2, CAP)
    share = lax.all_to_all(share, "expert", split_axis=0, concat_axis=0, tiled=True)
    sums = jnp.sum(given_sums + kept_sums, axis=(0, 3, 4))
    below, above = upward(sums), downward(sums)
    sums = (sums + upward(below)) + (below + above)
    factor = sums[:, 0] / (sums[:, 1] + epsilon)

    first, second = jnp.where(core == 0, z, x), jnp.where(core == 0, x, z)
    around = lambda value, sign: [(value + sign * shift) % 4 for shift in SHIFTS]
    held = jnp.stack([*around(first, -1), *around(second, 1), core, first]).astype(jnp.int32)
    where = jnp.stack([*around(second, -1), core, y]).astype(jnp.int32)
    gate, up = gate_values[0], up_values[0]

    def send(rows, before):
        return [rows[0]] + [
            move(after(rows[i], *before), False, SHIFTS[i], 0) for i in range(1, 4)
        ]

    rows = pick(1, after(held, factor, share), blocks)
    sent = send(rows, [])
    rows = pick(0, after(held, *rows), blocks)
    slot_weight = after(share, *rows).astype(jnp.float32).transpose(1, 0, 2).reshape(2, SLOTS, 1)
    weighted, their_weighted = weigh(core, gate, up, slot_weight)
    their_weighted = swap(after(their_weighted, *sent[1:]))

    def exchange(pieces):
        own, up_first, down_first, up_last, down_last = pieces
        return own, upward(up_first), downward(down_first), up_last, down_last

    def complete(pieces, *before):
        own, up_first, down_first, up_last, down_last = pieces
        up_last = upward(after(up_last, *before) + up_first[0])
        down_last = downward(after(down_last, *before) + down_first[1])
        return own, up_first, down_first, up_last, down_last

    own = send(rows, sent[1:])
    theirs = partial(False, where, their_weighted, sent)[0]
    before = grads(0, after(where, theirs), factor, effective, sent)[0]
    theirs = lax.psum_scatter(theirs, "dp", scatter_dimension=0, tiled=False)
    before = swap(after(before, *own[1:]))
    ours = exchange(partial(True, where, weighted, own))
    grad_gate, grad_up, scores = grads(
        1, where, factor, effective, own, (before, gate, up, slot_weight)
    )
    ours = complete(ours, scores)
    returned = lax.all_to_all(
        scores.reshape(2, SLOTS), "expert", split_axis=1, concat_axis=0, tiled=True
    )
    grad_route = back(expert_ids, rank, returned)
    summed = swap(theirs)
    grad_down = finish(where, factor, summed, ours)
    return (grad_gate[None], grad_up[None], grad_down, grad_route)


def solution(mesh):
    in_specs = (
        P(("dp", "expert"), None),
        P(("dp", "expert"), None),
        P(("dp", "expert"), None),
        P("dp", "expert", None, None),
        P("dp", "expert", None, None),
        P("expert", None, "dp"),
    )
    out_specs = (
        P("dp", "expert", None, None),
        P("dp", "expert", None, None),
        P("expert", None, "dp"),
        P(("dp", "expert"), None),
    )
    return jax.shard_map(
        on_device, mesh=mesh, in_specs=in_specs, out_specs=out_specs, check_vma=False
    )
```

```python
import functools

import jax
import jax.numpy as jnp
from jax import lax
from jax.experimental import pallas as pl
from jax.experimental.pallas import tpu as pltpu
from jax.sharding import PartitionSpec as P

epsilon = 1e-06

D = 4096
H = 768
TOP = 8
TOK = 256
CAP = 36
SLOTS = 1152
NZ = NX = 4
NDP = 4
PART = 2 * CAP
SEG = NZ * PART
UNIT = 256
HALF = 2 * UNIT
WIDE = NDP * HALF
SHIFTS = (0, 1, 3, 2)
VMEM_LIMIT = 56 * 1024 * 1024


def member(z, x, core):
    return ((z % NZ) * NX + (x % NX)) * 2 + core


def pairs(first_axis, shift, swap):
    out = []
    for z in range(NZ):
        for x in range(NX):
            for core in range(2):
                along_z = (core == 0) == first_axis
                to = (z + shift, x) if along_z else (z, x + shift)
                out.append((member(z, x, core), member(*to, core ^ swap)))
    return out


def params(**kw):
    return pltpu.CompilerParams(vmem_limit_bytes=VMEM_LIMIT, **kw)


def cost(flops, nbytes, trans=0):
    return pl.CostEstimate(flops=int(flops), bytes_accessed=int(nbytes), transcendentals=int(trans))


def shrink_kernel(half_ref, w_ref, out_ref, sums_ref):
    dense = w_ref[0].astype(jnp.float32).reshape(H // 8, 8, UNIT)
    row = lax.broadcasted_iota(jnp.int32, dense.shape, 1)
    odd = (row & 1) == 1
    high = (row & 2) == 2

    def across(value, step, upper):
        return jnp.where(upper, pltpu.roll(value, step, 1), pltpu.roll(value, 8 - step, 1))

    mag = jnp.abs(dense)
    other = across(mag, 1, odd)
    low, up = jnp.minimum(mag, other), jnp.maximum(mag, other)
    second = jnp.minimum(
        jnp.maximum(low, across(low, 2, high)), jnp.minimum(up, across(up, 2, high))
    )
    kept = jnp.maximum(mag - second, 0.0)
    shrunk = jnp.where(dense < 0.0, -kept, kept)
    out_ref[...] = shrunk.reshape(out_ref.shape).astype(jnp.bfloat16)

    def fold(value):
        value = jnp.sum(value, axis=0)
        return value[:, :128] + value[:, 128:]

    sums_ref[0, 0, 0] = fold(dense * shrunk)
    sums_ref[0, 0, 1] = fold(shrunk * shrunk)


def shrink(half, wide, w_down):
    if wide:
        spec = pl.BlockSpec((1, 1, H, UNIT), lambda e, t, s: (1, e, 0, t))
        shape = jax.ShapeDtypeStruct((2, 2, H, HALF), jnp.bfloat16)
    else:
        spec = pl.BlockSpec((1, H, UNIT), lambda e, t, s: (e, 0, t))
        shape = jax.ShapeDtypeStruct((2, H, HALF), jnp.bfloat16)
    return pl.pallas_call(
        shrink_kernel,
        grid_spec=pltpu.PrefetchScalarGridSpec(
            num_scalar_prefetch=1,
            grid=(2, 2),
            in_specs=[pl.BlockSpec((1, H, UNIT), lambda e, t, s: (e, 0, 2 * s[0] + t))],
            out_specs=[spec, pl.BlockSpec((1, 1, 2, 8, 128), lambda e, t, s: (t, e, 0, 0, 0))],
        ),
        out_shape=[shape, jax.ShapeDtypeStruct((2, 2, 2, 8, 128), jnp.float32)],
        compiler_params=params(),
        cost_estimate=cost(2 * H * HALF * 30, 2 * 2 * H * HALF * 2),
        name="shrink",
    )(half.reshape(1).astype(jnp.int32), w_down)


def back_kernel(ids_ref, rank_ref, score_ref, out_ref):
    expert = lax.broadcasted_iota(jnp.int32, (64, TOK), 0)
    rank = rank_ref[...]
    score = jnp.zeros((64, TOK), jnp.float32)
    for slot in range(CAP):
        score = jnp.where(rank == float(slot), score_ref[:, slot : slot + 1], score)
    for k in range(TOP):
        hit = ids_ref[k : k + 1, :] == expert
        out_ref[k : k + 1, :] = jnp.sum(jnp.where(hit, score, 0.0), axis=0, keepdims=True)


def back(ids, rank, score):
    out = pl.pallas_call(
        back_kernel,
        out_shape=jax.ShapeDtypeStruct((TOP, TOK), jnp.float32),
        compiler_params=params(),
        name="back",
    )(ids.T, rank, score)
    return out.T


def split_kernel(core_ref, rows_ref, ids_ref, weights_ref, mine_ref, theirs_ref, share_ref, rank_ref):
    core = core_ref[0]
    owner = pl.program_id(0)

    @pl.when(owner == 0)
    def _():
        expert = lax.broadcasted_iota(jnp.int32, (64, TOK), 0)
        named = jnp.zeros((64, TOK), jnp.float32)
        weight = jnp.zeros((64, TOK), jnp.float32)
        for k in range(TOP):
            hit = ids_ref[k : k + 1, :] == expert
            named = jnp.where(hit, 1.0, named)
            weight = jnp.where(hit, weights_ref[k : k + 1, :], weight)
        earlier = lax.broadcasted_iota(jnp.int32, (TOK, TOK), 0) < lax.broadcasted_iota(
            jnp.int32, (TOK, TOK), 1
        )
        rank = jnp.dot(
            named.astype(jnp.bfloat16),
            jnp.where(earlier, 1.0, 0.0).astype(jnp.bfloat16),
            preferred_element_type=jnp.float32,
        )
        rank = jnp.where(named > 0.0, rank, -1.0)
        rank_ref[...] = rank
        lane = lax.broadcasted_iota(jnp.int32, (64, 128), 1)
        share = jnp.zeros((64, 128), jnp.float32)
        for slot in range(CAP):
            one = jnp.sum(jnp.where(rank == float(slot), weight, 0.0), axis=1, keepdims=True)
            share = jnp.where(lane == slot, one, share)
        share_ref[...] = share.astype(jnp.bfloat16)

    ranks = rank_ref[pl.ds(pl.multiple_of(owner * 16, 16), 16), :].astype(jnp.bfloat16)
    ranks = jnp.concatenate([ranks, jnp.zeros_like(ranks)], axis=1)
    columns = lambda half: pl.ds(pl.multiple_of(half * HALF, HALF), HALF)
    mine_ref[0, :TOK, :] = rows_ref[:, columns(core)]
    theirs_ref[:TOK, :] = rows_ref[:, columns(1 - core)]
    mine_ref[0, TOK:, :] = ranks
    theirs_ref[TOK:, :] = ranks


def split(core, rows, ids, weights):
    deep = TOK + 16
    small = pl.BlockSpec((TOP, TOK), lambda j, s: (0, 0))
    return pl.pallas_call(
        split_kernel,
        grid_spec=pltpu.PrefetchScalarGridSpec(
            num_scalar_prefetch=1,
            grid=(NDP,),
            in_specs=[pl.BlockSpec((TOK, 1024), lambda j, s: (0, j)), small, small],
            out_specs=[
                pl.BlockSpec((1, deep, HALF), lambda j, s: (s[0], 0, j)),
                pl.BlockSpec((deep, HALF), lambda j, s: (0, j)),
                pl.BlockSpec((64, 128), lambda j, s: (0, 0)),
                pl.BlockSpec((64, TOK), lambda j, s: (0, 0)),
            ],
        ),
        out_shape=[
            jax.ShapeDtypeStruct((2, deep, WIDE), jnp.bfloat16),
            jax.ShapeDtypeStruct((deep, WIDE), jnp.bfloat16),
            jax.ShapeDtypeStruct((64, 128), jnp.bfloat16),
            jax.ShapeDtypeStruct((64, TOK), jnp.float32),
        ],
        compiler_params=params(),
        name="split",
    )(core.reshape(1).astype(jnp.int32), rows, ids.T, weights.astype(jnp.float32).T)


def held_by(buffers, to, e):
    return buffers[2 * to - 1 + e] if to in (1, 2) else buffers[min(to * 2, 5)].at[e]


def pick_kernel(swap, where_ref, *refs):
    outs = refs[5:11]
    tokens, coded, ranks, onehot, picked, sems = refs[11:]
    blocks = [[ref.at[part] for part in range(2)] for ref in refs[:3]] + [refs[3:5]]
    step = pl.program_id(0)
    core = where_ref[8]

    def tile(n):
        columns = pl.ds(pl.multiple_of(n * HALF, HALF), HALF)
        return [
            pltpu.make_async_copy(
                blocks[i][part].at[pl.ds(0, TOK), columns],
                tokens.at[n, where_ref[i], pl.ds(part * TOK, TOK)],
                sems.at[n, 2 * i + part],
            )
            for i in range(4)
            for part in range(2)
        ]

    @pl.when(step == 0)
    def _():
        plane = [jnp.where(core == 0, where_ref[9], where_ref[4 + i]) for i in range(4)]
        inside = [jnp.where(core == 0, where_ref[4 + i], where_ref[9]) for i in range(4)]
        tables = [
            pltpu.make_async_copy(
                blocks[i][part].at[pl.ds(TOK, 16)], coded.at[where_ref[i], part], sems.at[4, 2 * i + part]
            )
            for i in range(4)
            for part in range(2)
        ]
        for copy in tables:
            copy.start()
        for n in range(4):
            for copy in tile(n):
                copy.start()
        for copy in tables:
            copy.wait()
        for block in range(4):
            for part in range(2):
                ranks[block, part] = coded[block, part].astype(jnp.float32)
        row = lax.broadcasted_iota(jnp.int32, (PART, 2 * TOK), 0)
        lane = lax.broadcasted_iota(jnp.int32, (PART, 2 * TOK), 1)
        second = row >= CAP
        slot = jnp.where(second, row - CAP, row)
        slot = jnp.where(second == (lane >= TOK), slot, -2).astype(jnp.float32)
        for i in range(8):
            to, e = i // 2, i % 2
            at = inside[to] * 4 + jnp.where(core == swap, 0, 2) + e
            columns = pl.ds(pl.multiple_of(plane[to] * HALF, HALF), TOK)
            for block in range(4):
                rank = jnp.concatenate(
                    [ranks[block, part, pl.ds(at, 1), columns] for part in range(2)], axis=1
                )
                onehot[block, i * PART : (i + 1) * PART, :] = jnp.where(
                    slot == rank, 1.0, 0.0
                ).astype(jnp.bfloat16)

    for copy in tile(step):
        copy.wait()
    for block in range(4):
        picked[block] = jnp.dot(
            onehot[block], tokens[step, block], preferred_element_type=jnp.float32
        )
    for i in range(8):
        rows = pl.ds(i * PART, PART)
        joined = jnp.concatenate([picked[block, rows, :] for block in range(4)], axis=0)
        held_by(outs, i // 2, i % 2)[...] = joined.astype(jnp.bfloat16)


def pick(swap, where, blocks):
    pair = pl.BlockSpec((2, SEG, HALF), lambda n, s: (0, 0, n))
    single = pl.BlockSpec((SEG, HALF), lambda n, s: (0, n))
    any_spec = pl.BlockSpec(memory_space=pl.ANY)
    return pl.pallas_call(
        functools.partial(pick_kernel, swap),
        grid_spec=pltpu.PrefetchScalarGridSpec(
            num_scalar_prefetch=1,
            grid=(4,),
            in_specs=[any_spec] * 5,
            out_specs=[pair] + [single] * 4 + [pair],
            scratch_shapes=[
                pltpu.VMEM((4, 4, 2 * TOK, HALF), jnp.bfloat16),
                pltpu.VMEM((4, 2, 16, WIDE), jnp.bfloat16),
                pltpu.VMEM((4, 2, 16, WIDE), jnp.float32),
                pltpu.VMEM((4, 8 * PART, 2 * TOK), jnp.bfloat16),
                pltpu.VMEM((4, 8 * PART, HALF), jnp.float32),
                pltpu.SemaphoreType.DMA((5, 8)),
            ],
        ),
        out_shape=[
            jax.ShapeDtypeStruct((2, SEG, WIDE) if n in (0, 5) else (SEG, WIDE), jnp.bfloat16) for n in range(6)
        ],
        compiler_params=params(),
        cost_estimate=cost(2 * 4 * 576 * 512 * WIDE, 8 * TOK * WIDE * 2 + 8 * SEG * WIDE * 2),
        name=f"pick{1 - swap}",
    )(where, *blocks)


def weigh_kernel(core_ref, gate_ref, up_ref, weight_ref, mine_ref, theirs_ref):
    gate = gate_ref[0].astype(jnp.float32)
    up = up_ref[0].astype(jnp.float32)
    sig = 0.5 * jnp.tanh(0.5 * gate) + 0.5
    value = weight_ref[0] * (gate * sig * up)
    turned = jnp.concatenate(
        [
            value[(z * NX + x) * PART : (z * NX + x + 1) * PART]
            for x in range(NX)
            for z in range(NZ)
        ],
        axis=0,
    )
    plain, turned = value.astype(jnp.bfloat16).T, turned.astype(jnp.bfloat16).T

    @pl.when(core_ref[0] == 0)
    def _():
        mine_ref[0] = turned
        theirs_ref[0] = plain

    @pl.when(core_ref[0] == 1)
    def _():
        mine_ref[0] = plain
        theirs_ref[0] = turned


def weigh(core, gate, up, slot_weight):
    wide = 256
    column = pl.BlockSpec((1, SLOTS, wide), lambda e, n, s: (e, 0, n))
    out = pl.BlockSpec((1, wide, SLOTS), lambda e, n, s: (e, n, 0))
    return pl.pallas_call(
        weigh_kernel,
        grid_spec=pltpu.PrefetchScalarGridSpec(
            num_scalar_prefetch=1,
            grid=(2, H // wide),
            in_specs=[column, column, pl.BlockSpec((1, SLOTS, 1), lambda e, n, s: (e, 0, 0))],
            out_specs=[out, out],
        ),
        out_shape=[jax.ShapeDtypeStruct((2, H, SLOTS), jnp.bfloat16)] * 2,
        compiler_params=params(),
        cost_estimate=cost(2 * SLOTS * H * 20, 2 * SLOTS * H * 8, 2 * SLOTS * H),
        name="weigh",
    )(core.reshape(1).astype(jnp.int32), gate, up, slot_weight)


OWNERS = (0, 1, 3, 2)
DEPTH = 3


def segment(where_ref, i):
    return pl.ds(pl.multiple_of(where_ref[i] * SEG, SEG), SEG)


def partial_kernel(ring, where_ref, weighted_ref, *refs):
    buffers, outs = refs[:6], refs[6:-6]
    weights, rows, ready, weight_sems, in_sems, out_sems = refs[-6:]
    steps = [(i, j) for i in range(2) for j in (3, 1, 2, 0)]

    def load(s):
        i, j = steps[s]
        at = lax.rem(where_ref[5] + OWNERS[j], NDP) if ring else j
        columns = pl.ds(pl.multiple_of(at * HALF, HALF), HALF)
        return [
            pltpu.make_async_copy(
                held_by(buffers, r, i).at[:, columns],
                rows.at[s % DEPTH, segment(where_ref, r)],
                in_sems.at[s % DEPTH, r],
            )
            for r in range(4)
        ]

    def store(s):
        i, j = steps[s]
        if ring:
            own, up_first, down_first, up_last, down_last = outs
            to = {
                0: [own.at[0, i], own.at[1, i]],
                1: [up_last.at[i], up_first.at[1, i]],
                2: [down_first.at[0, i], down_last.at[i]],
                3: [up_first.at[0, i], down_first.at[1, i]],
            }[j]
        else:
            to = [outs[0].at[j, p, i] for p in range(2)]
        return [
            pltpu.make_async_copy(ready.at[s % 2, p], to[p], out_sems.at[s % 2, p]) for p in range(2)
        ]

    fetch = [
        pltpu.make_async_copy(weighted_ref.at[i], weights.at[i], weight_sems.at[i]) for i in range(2)
    ]
    fetch[0].start()
    for s in range(DEPTH):
        for copy in load(s):
            copy.start()
    for copy in fetch[1:]:
        copy.start()
    for s in range(len(steps)):
        i, j = steps[s]
        if s % NDP == 0:
            fetch[i].wait()
        for copy in load(s):
            copy.wait()
        if s >= 2:
            for copy in store(s - 2):
                copy.wait()
        for p in range(2):
            ready[s % 2, p] = jnp.dot(
                weights[i],
                rows[s % DEPTH, :, p * UNIT : (p + 1) * UNIT],
                preferred_element_type=jnp.float32,
            ).astype(jnp.bfloat16)
        for copy in store(s):
            copy.start()
        if s + DEPTH < len(steps):
            for copy in load(s + DEPTH):
                copy.start()
    for s in range(len(steps) - 2, len(steps)):
        for copy in store(s):
            copy.wait()


def partial(ring, where, weighted, buffers):
    any_spec = pl.BlockSpec(memory_space=pl.ANY)
    shapes = [(2, 2, H, UNIT)] * 3 + [(2, H, UNIT)] * 2 if ring else [(NDP, 2, 2, H, UNIT)]
    return pl.pallas_call(
        functools.partial(partial_kernel, ring),
        grid_spec=pltpu.PrefetchScalarGridSpec(
            num_scalar_prefetch=1,
            grid=(1,),
            in_specs=[any_spec] * (1 + len(buffers)),
            out_specs=[any_spec] * len(shapes),
            scratch_shapes=[
                pltpu.VMEM((2, H, SLOTS), jnp.bfloat16),
                pltpu.VMEM((DEPTH, SLOTS, HALF), jnp.bfloat16),
                pltpu.VMEM((2, 2, H, UNIT), jnp.bfloat16),
                pltpu.SemaphoreType.DMA((2,)),
                pltpu.SemaphoreType.DMA((DEPTH, 4)),
                pltpu.SemaphoreType.DMA((2, 2)),
            ],
        ),
        out_shape=[jax.ShapeDtypeStruct(shape, jnp.bfloat16) for shape in shapes],
        compiler_params=params(),
        cost_estimate=cost(
            2 * 2 * SLOTS * H * WIDE, 2 * (SLOTS * WIDE * 2 + H * WIDE * 2 + H * SLOTS * 2)
        ),
        name="partial",
    )(where, weighted, *buffers)


def grads_kernel(group, where_ref, factor_ref, effective_ref, *refs):
    buffers, refs = refs[:6], refs[6:]
    rows, eff, total, sems = refs[-4:]
    e = pl.program_id(0)

    def load(at, k):
        return [
            pltpu.make_async_copy(
                held_by(buffers, r, at).at[:, pl.ds(k * 1024, 1024)],
                rows.at[k, segment(where_ref, r)],
                sems.at[k, r],
            )
            for r in range(4)
        ] + [
            pltpu.make_async_copy(
                effective_ref.at[2 * k + j, group, at],
                eff.at[k, :, pl.ds(j * HALF, HALF)],
                sems.at[k, 4 + j],
            )
            for j in range(2)
        ]

    @pl.when(e == 0)
    def _():
        for k in range(2):
            for copy in load(0, k):
                copy.start()

    for k in range(2):
        for copy in load(0, k):
            copy.wait()
        for n in range(H // 256):
            columns = slice(n * 256, (n + 1) * 256)
            value = lax.dot_general(
                rows[k], eff[k, columns, :], (((1,), (1,)), ((), ())), preferred_element_type=jnp.float32
            )
            if k == 0:
                total[:, columns] = value
            else:
                total[:, columns] += value

        @pl.when(e == 0)
        def _(k=k):
            for copy in load(1, k):
                copy.start()

    def piece(i, carry):
        at = pl.ds(pl.multiple_of(i * 2 * PART, 2 * PART), 2 * PART)
        z = i // 2
        x = (i - z * 2) * 2
        source = [jnp.where(where_ref[4] == 0, (x + k) * NZ + z, 2 * i + k) for k in range(2)]
        product = jnp.concatenate(
            [total[pl.ds(pl.multiple_of(one * PART, PART), PART), :] for one in source], axis=0
        )
        if not group:
            refs[0][0, at, :] = product
            return carry
        before_ref, gate_ref, up_ref, weight_ref, gate_out, up_out, score_out = refs[:7]
        slot_grads = factor_ref[e] * (before_ref[0, at, :] + product)
        gate = gate_ref[0, at, :].astype(jnp.float32)
        up = up_ref[0, at, :].astype(jnp.float32)
        sig = 0.5 * jnp.tanh(0.5 * gate) + 0.5
        activated = gate * sig
        score_out[0, at, :] = jnp.sum(slot_grads * (activated * up), axis=1, keepdims=True)
        scaled = weight_ref[0, at, :] * slot_grads
        gate_out[0, at, :] = (scaled * up * (sig + activated * (1.0 - sig))).astype(jnp.bfloat16)
        up_out[0, at, :] = (scaled * activated).astype(jnp.bfloat16)
        return carry

    lax.fori_loop(0, SLOTS // (2 * PART), piece, 0)


def grads(group, where, factor, effective, buffers, others=()):
    any_spec = pl.BlockSpec(memory_space=pl.ANY)
    block = pl.BlockSpec((1, SLOTS, H), lambda n, s, f: (n, 0, 0))
    column = pl.BlockSpec((1, SLOTS, 1), lambda n, s, f: (n, 0, 0))
    shape = lambda dtype, width=H: jax.ShapeDtypeStruct((2, SLOTS, width), dtype)
    if group:
        ins, outs = [block, block, block, column], [block, block, column]
        shapes = [shape(jnp.bfloat16), shape(jnp.bfloat16), shape(jnp.float32, 1)]
    else:
        ins, outs, shapes = [], [block], [shape(jnp.float32)]
    return pl.pallas_call(
        functools.partial(grads_kernel, group),
        grid_spec=pltpu.PrefetchScalarGridSpec(
            num_scalar_prefetch=2,
            grid=(2,),
            in_specs=[any_spec] * 7 + ins,
            out_specs=outs,
            scratch_shapes=[
                pltpu.VMEM((2, SLOTS, 1024), jnp.bfloat16),
                pltpu.VMEM((2, H, 1024), jnp.bfloat16),
                pltpu.VMEM((SLOTS, H), jnp.float32),
                pltpu.SemaphoreType.DMA((2, 6)),
            ],
        ),
        out_shape=shapes,
        compiler_params=params(),
        cost_estimate=cost(
            2 * 2 * SLOTS * H * WIDE + group * 2 * SLOTS * H * 30,
            2 * (SLOTS * WIDE * 2 + H * WIDE * 2 + SLOTS * H * (12 if group else 4)),
        ),
        name=f"grads{group}",
    )(where, factor, effective, *buffers, *others)


def collect(own, up, down, low, high):
    wide = lambda value: value.astype(jnp.float32)
    return (
        wide(own[0, 0]) + (wide(low[0]) + wide(down[0, 0])),
        wide(own[1, 0]) + (wide(up[1, 0]) + wide(high[0])),
    )


PAIR = pl.BlockSpec((2, 1, H, UNIT), lambda n, *s: (0, n, 0, 0))
SINGLE = pl.BlockSpec((1, H, UNIT), lambda n, *s: (n, 0, 0))


def finish_kernel(where_ref, factor_ref, theirs, *refs):
    out_ref = refs[5]
    core = where_ref[4]
    factor = factor_ref[pl.program_id(0)]
    for p, value in enumerate(collect(*refs[:5])):
        mine = pl.ds(pl.multiple_of(core * HALF + p * UNIT, UNIT), UNIT)
        other = pl.ds(pl.multiple_of((1 - core) * HALF + p * UNIT, UNIT), UNIT)
        out_ref[0, :, mine] = (factor * value).astype(jnp.bfloat16)
        out_ref[0, :, other] = (factor * theirs[p, 0].astype(jnp.float32)).astype(jnp.bfloat16)


def finish(where, factor, theirs, pieces):
    return pl.pallas_call(
        finish_kernel,
        grid_spec=pltpu.PrefetchScalarGridSpec(
            num_scalar_prefetch=2,
            grid=(2,),
            in_specs=[PAIR] * 4 + [SINGLE] * 2,
            out_specs=pl.BlockSpec((1, H, 1024), lambda n, *s: (n, 0, 0)),
        ),
        out_shape=jax.ShapeDtypeStruct((2, H, 1024), jnp.bfloat16),
        compiler_params=params(),
        name="finish",
    )(where, factor, theirs, *pieces)


def after(value, *first):
    return lax.optimization_barrier((value, *first))[0]


def on_device(grad_out, expert_ids, route_weights, gate_values, up_values, w_down):
    me = lax.axis_index("expert")
    y = lax.axis_index("dp")
    core = me % 2
    x = (me // 2) % NX
    z = me // (2 * NX)
    move = lambda value, *to: lax.ppermute(value, "expert", pairs(*to))
    swap = lambda value: move(value, True, 0, 1)
    upward = lambda value: lax.ppermute(value, "dp", [(i, (i + 1) % NDP) for i in range(NDP)])
    downward = lambda value: lax.ppermute(value, "dp", [(i, (i - 1) % NDP) for i in range(NDP)])

    mine, theirs, share, rank = split(core, grad_out, expert_ids, route_weights)
    partner = swap(theirs)
    given, given_sums = shrink(1 - core, False, after(w_down, theirs))
    block = lax.dynamic_update_slice(mine, partner[None], (1 - core, 0, 0))
    block = after(block, given)
    blocks = [block, move(block, True, 1, 0), move(block, True, -1, 0)]
    blocks += [move(blocks[1][0], True, 1, 0), move(blocks[2][1], True, -1, 0)]
    kept, kept_sums = shrink(core, True, after(w_down, upward(given_sums)))
    effective = lax.dynamic_update_slice(kept, swap(given)[None], (0, 0, 0, 0))
    effective = lax.all_gather(effective, "dp", axis=0)

    share = share[:, :CAP].reshape(NZ * NX * 2, 2, CAP)
    share = lax.all_to_all(share, "expert", split_axis=0, concat_axis=0, tiled=True)
    sums = jnp.sum(given_sums + kept_sums, axis=(0, 3, 4))
    below, above = upward(sums), downward(sums)
    sums = (sums + upward(below)) + (below + above)
    factor = sums[:, 0] / (sums[:, 1] + epsilon)

    first, second = jnp.where(core == 0, z, x), jnp.where(core == 0, x, z)
    around = lambda value, sign: [(value + sign * shift) % 4 for shift in SHIFTS]
    held = jnp.stack([*around(first, -1), *around(second, 1), core, first]).astype(jnp.int32)
    where = jnp.stack([*around(second, -1), core, y]).astype(jnp.int32)
    gate, up = gate_values[0], up_values[0]

    def send(rows, before):
        along = (0, 1, 1, 2, 2, 3)
        return [rows[0]] + [
            move(after(rows[i], *before), False, SHIFTS[along[i]], 0) for i in range(1, 6)
        ]

    rows = pick(1, after(held, factor, share), blocks)
    sent = send(rows, [])
    rows = pick(0, after(held, *rows), blocks)
    slot_weight = after(share, *rows).astype(jnp.float32).transpose(1, 0, 2).reshape(2, SLOTS, 1)
    weighted, their_weighted = weigh(core, gate, up, slot_weight)
    their_weighted = swap(after(their_weighted, *sent[1:]))

    def exchange(pieces):
        own, up_first, down_first, up_last, down_last = pieces
        return own, upward(up_first), downward(down_first), up_last, down_last

    def complete(pieces, *before):
        own, up_first, down_first, up_last, down_last = pieces
        up_last = upward(after(up_last, *before) + up_first[0])
        down_last = downward(after(down_last, *before) + down_first[1])
        return own, up_first, down_first, up_last, down_last

    own = send(rows, sent[1:])
    theirs = partial(False, where, their_weighted, sent)[0]
    before = grads(0, after(where, theirs), factor, effective, sent)[0]
    theirs = lax.psum_scatter(after(theirs, own[1], own[3]), "dp", scatter_dimension=0, tiled=False)
    before = swap(after(before, *own[1:]))
    ours = exchange(partial(True, where, weighted, own))
    grad_gate, grad_up, scores = grads(
        1, where, factor, effective, own, (before, gate, up, slot_weight)
    )
    ours = complete(ours, scores)
    returned = lax.all_to_all(
        scores.reshape(2, SLOTS), "expert", split_axis=1, concat_axis=0, tiled=True
    )
    grad_route = back(expert_ids, rank, returned)
    summed = swap(after(theirs, scores))
    grad_down = finish(where, factor, summed, ours)
    return (grad_gate[None], grad_up[None], grad_down, grad_route)


def solution(mesh):
    in_specs = (
        P(("dp", "expert"), None),
        P(("dp", "expert"), None),
        P(("dp", "expert"), None),
        P("dp", "expert", None, None),
        P("dp", "expert", None, None),
        P("expert", None, "dp"),
    )
    out_specs = (
        P("dp", "expert", None, None),
        P("dp", "expert", None, None),
        P("expert", None, "dp"),
        P(("dp", "expert"), None),
    )
    return jax.shard_map(
        on_device, mesh=mesh, in_specs=in_specs, out_specs=out_specs, check_vma=False
    )
```
